256 devices in a mesh: board: 32 (over y_hi, z, core), hist: 4 (over x), pair: 2 (over y_lo).
Axes of the slice: x: 4, y: 4 (y_hi: 2, y_lo: 2; y = y_hi * 2 + y_lo), z: 8, core: 2. Of those that a mesh axis runs over, the one named last changes fastest.
Arguments:
- turn_reach: bfloat16 [2, 2048, 4, 256], P('pair', 'board', None, 'hist'), may hold values from 0.0099487305 to 1
- regrets: float32 [2, 32, 256, 2048], P('pair', 'board', 'hist'), may hold values from -6 to 6
- pot: float32 [256], P('hist'), may hold values from 0.5 to 4
- turn_cluster: int32 [32], P('board'), may hold values from 0 to 3
- bucket_map: int32 [32, 2048], P('board'), may hold values from 0 to 2047
- codes: int32 [256], P('hist'), may hold values from 0 to 2, as said below
- ranks: int32 [32, 2048], P('board'), may hold values from 0 to 2047
Outputs:
- new_regrets: float32 [2, 32, 256, 2048], P('pair', 'board', 'hist')
- turn_values: float32 [2, 2048, 4, 256], P('pair', 'board', None, 'hist')
The draws below stay inside these ranges and needn't reach their ends.
Inputs may be any that keep to these rules, and one draw needn't show every extreme that they name: `codes`: 0: player 0 folded, 1: player 1 folded, 2: showdown; a function of the history alone: among the 4 siblings of each node exactly one is a fold (0 or 1), the others are 2. Equal ranks tie.
All inputs are finite; a program needn't handle non-finite values.
Results may differ from the reference program's by a relative error of at most 0.0018.
Values may be sent and summed in bfloat16 or wider, within the bound.
A program may use at most 64 MiB of HBM per device.

```python
import math
import jax
import jax.numpy as jnp
from jax import lax

KR = 2048
KT = 2048
H = 256
ACTIONS = 4
TC = 4
B = 32


def draw_codes(key, part):
    key = jax.random.fold_in(key, 5)
    nodes = H // ACTIONS
    first, second = jax.random.split(key)
    fold_at = jax.random.randint(first, (nodes,), 0, ACTIONS)
    folder = jax.random.randint(second, (nodes,), 0, 2)
    action = jnp.arange(H, dtype=jnp.int32) // nodes
    node_of = jnp.arange(H, dtype=jnp.int32) % nodes
    return jnp.where(action == fold_at[node_of], folder[node_of], 2).astype(jnp.int32)


def place_ends(result, key, smallest, largest):
    index_at = [jax.random.randint(jax.random.fold_in(key, axis), (), 0, length) for axis, length in enumerate(result.shape)]
    widest = result.shape.index(max(result.shape))
    neighbour = index_at[:widest] + [(index_at[widest] + 1) % result.shape[widest]] + index_at[widest + 1:]
    return result.at[tuple(index_at)].set(smallest).at[tuple(neighbour)].set(largest)


def levels(rng, dims, shards, low, top_value):
    def one(position, shards_of):
        heights = jax.random.uniform(jax.random.fold_in(jax.random.fold_in(rng, 6), position), (shards_of,), jnp.float32, low / len(shards), top_value / len(shards))
        return jnp.repeat(jnp.exp(heights), dims[position] // shards_of).reshape((-1,) + (1,) * (len(dims) - position - 1))

    factor_of = one(*shards[0])
    for cut in shards[1:]:
        factor_of = factor_of * one(*cut)
    return factor_of


def bell_draw(rng, extent, spread, limit, shards=(), held_as=jnp.bfloat16):
    entries = jax.random.normal(rng, extent, jnp.float32) * spread
    if len(shards) > 0:
        entries = levels(rng, extent, shards, -0.22, 0.18) * entries
    return jnp.clip(entries, min=-limit, max=limit).astype(held_as)


def setup_inputs(seed: int = 0) -> dict:
    splits = jax.random.split(jax.random.key(seed), 8)
    turn_reach = jnp.clip(jnp.exp(math.log(1.0) - 4.61031033 * jax.random.uniform(splits[0], (2, KT, TC, H), jnp.float32) ** levels(splits[0], (2, KT, TC, H), ((0, 2), (1, 32), (3, 4)), -0.2, 0.2)), 0.0099487305, 1.0).astype(jnp.bfloat16)
    regrets = bell_draw(splits[1], (2, B, H, KR), 1.0, 6.0, ((0, 2), (1, 32), (2, 4)), jnp.float32)
    pot = jnp.clip(jnp.exp(math.log(4.0) - 2.0794415 * jax.random.uniform(splits[2], (H,), jnp.float32) ** levels(splits[2], (H,), ((0, 4),), -0.2, 0.2)), 0.5, 4.0)
    turn_cluster = place_ends(jax.random.randint(splits[3], (B,), 0, TC), jax.random.fold_in(splits[3], 1), 0, TC - 1).astype(jnp.int32)
    bucket_map = place_ends(jax.random.randint(splits[4], (B, KR), 0, KT), jax.random.fold_in(splits[4], 1), 0, KT - 1).astype(jnp.int32)
    codes = draw_codes(jax.random.fold_in(splits[7], 71), 0)
    ranks = place_ends(jax.random.randint(splits[6], (B, KR), 0, KR), jax.random.fold_in(splits[6], 1), 0, KR - 1).astype(jnp.int32)
    return dict(turn_reach=turn_reach, regrets=regrets, pot=pot, turn_cluster=turn_cluster, bucket_map=bucket_map, codes=codes, ranks=ranks)


SMOOTH = 0.01


def regret_match(regret_board):
    grouped = regret_board.reshape(2, ACTIONS, H // ACTIONS, KR)
    positive = jnp.maximum(grouped, 0.0)
    total = jnp.sum(positive, axis=1, keepdims=True)
    return ((positive + SMOOTH) / (total + ACTIONS * SMOOTH)).reshape(2, H, KR)


def reference(turn_reach, regrets, pot, turn_cluster, bucket_map, codes, ranks):
    scale = KR ** -0.5
    player = jnp.arange(2, dtype=jnp.int32)[:, None]
    signs = jnp.where(codes[None, :] == player, -1.0, 1.0).astype(jnp.float32)
    is_show = (codes == 2)[None, :, None]

    def board_step(accum, items):
        regret_board, cluster, mapping, rank = items
        sigma = regret_match(regret_board)
        panel = lax.dynamic_index_in_dim(turn_reach, cluster, axis=2, keepdims=False)
        lifted = jnp.take(panel, mapping, axis=1).astype(jnp.float32).transpose(0, 2, 1)
        reach = (lifted * sigma).astype(jnp.bfloat16)
        strength = jnp.sign(rank[:, None] - rank[None, :]).astype(jnp.float32)
        flat = reach.astype(jnp.float32).reshape(2 * H, KR)
        showdown = jnp.dot(flat, strength.T, precision=lax.Precision.HIGHEST).reshape(2, H, KR)
        totals = jnp.sum(reach.astype(jnp.float32), axis=2)
        opp_show = showdown[::-1]
        opp_total = totals[::-1]
        fold = (signs * pot[None, :] * scale * opp_total)[:, :, None]
        show = pot[None, :, None] * scale * opp_show
        value = jnp.where(is_show, show, fold)
        weighted = sigma * value
        node = jnp.sum(weighted.reshape(2, ACTIONS, H // ACTIONS, KR), axis=1, keepdims=True)
        updated = (regret_board.reshape(2, ACTIONS, H // ACTIONS, KR) + value.reshape(2, ACTIONS, H // ACTIONS, KR) - node).reshape(2, H, KR)
        carried = weighted.astype(jnp.bfloat16).astype(jnp.float32)
        contrib = jax.ops.segment_sum(carried.transpose(2, 0, 1), mapping, num_segments=KT)
        accum = accum.at[:, :, cluster, :].add(contrib.transpose(1, 0, 2))
        return accum, updated

    start = jnp.zeros((2, KT, TC, H), jnp.float32)
    accum, updated = lax.scan(board_step, start, (regrets.transpose(1, 0, 2, 3), turn_cluster, bucket_map, ranks))
    return updated.transpose(1, 0, 2, 3), accum
```

```python
import functools

import jax
import jax.numpy as jnp
from jax import lax
from jax.experimental import pallas as pl
from jax.experimental.pallas import tpu as pltpu
from jax.sharding import PartitionSpec as P

ACTIONS = 4
CLUSTERS = 4
PLAYERS = 2
SMOOTH = 0.01
CHUNK = 8
SLOTS = PLAYERS * ACTIONS
ROWS = SLOTS * CHUNK
HALVES = 2
PIECE = 64
LANES = 128
MESH = pl.DeviceIdType.MESH


def kernel(
    ring,
    regrets,
    turn,
    pot,
    codes,
    cluster,
    mapping,
    ranks,
    fresh,
    shares,
    onehot,
    strength,
    meta_out,
    meta,
    regret,
    sigma,
    near,
    cluster_out,
    clusters,
    far_out,
    far,
    reach,
    updated,
    weighted,
    back_out,
    back,
    last_out,
    last,
    regret_send,
    regret_recv,
    meta_send,
    meta_recv,
    near_send,
    near_recv,
    cluster_send,
    cluster_recv,
    far_send,
    far_recv,
    fresh_send,
    fresh_recv,
    back_send,
    back_recv,
    last_send,
    last_recv,
    local_sem,
):
    width = ranks.shape[1]
    depth = ring * LANES
    board = lax.axis_index("board")
    action = lax.axis_index("hist")
    player = lax.axis_index("pair")
    half = board // ring
    place = board % ring
    chunk = action * PLAYERS + player
    slot = player * ACTIONS + action
    group = half * SLOTS + chunk
    scale = width ** (-0.5)

    def same_board(step):
        other = (chunk + step) % SLOTS
        return other, {"board": board, "hist": other // PLAYERS, "pair": other % PLAYERS}

    def near_peer(step):
        other = (group + step) % (HALVES * SLOTS)
        their_chunk = other % SLOTS
        target = {
            "board": (other // SLOTS) * ring + place,
            "hist": their_chunk // PLAYERS,
            "pair": their_chunk % PLAYERS,
        }
        return other, target

    def far_peer(step):
        other = (place + step) % ring
        return other, {"board": half * ring + other, "hist": action, "pair": player}

    def regret_copy(step):
        other, target = same_board(step)
        return pltpu.make_async_remote_copy(
            src_ref=regrets.at[pl.ds(pl.multiple_of(other * CHUNK, CHUNK), CHUNK)],
            dst_ref=regret.at[slot],
            send_sem=regret_send.at[step],
            recv_sem=regret_recv.at[step],
            device_id=target,
            device_id_type=MESH,
        )

    def meta_copy(step):
        other, target = same_board(step)
        return pltpu.make_async_remote_copy(
            src_ref=meta_out.at[other],
            dst_ref=meta.at[slot],
            send_sem=meta_send.at[step],
            recv_sem=meta_recv.at[step],
            device_id=target,
            device_id_type=MESH,
        )

    def near_copy(step):
        other, target = near_peer(step)
        return pltpu.make_async_remote_copy(
            src_ref=turn.at[other % SLOTS],
            dst_ref=near.at[half * SLOTS + slot],
            send_sem=near_send.at[step],
            recv_sem=near_recv.at[step],
            device_id=target,
            device_id_type=MESH,
        )

    def cluster_copy(step):
        other, target = far_peer(step)
        return pltpu.make_async_remote_copy(
            src_ref=cluster_out,
            dst_ref=clusters.at[place],
            send_sem=cluster_send.at[step],
            recv_sem=cluster_recv.at[step],
            device_id=target,
            device_id_type=MESH,
        )

    def far_copy(step):
        other, target = far_peer(step)
        return pltpu.make_async_remote_copy(
            src_ref=far_out.at[other],
            dst_ref=far.at[:, pl.ds(pl.multiple_of(place * LANES, LANES), LANES)],
            send_sem=far_send.at[step],
            recv_sem=far_recv.at[step],
            device_id=target,
            device_id_type=MESH,
        )

    def fresh_copy(step):
        other, target = same_board(step)
        their_slot = (other % PLAYERS) * ACTIONS + other // PLAYERS
        return pltpu.make_async_remote_copy(
            src_ref=updated.at[their_slot],
            dst_ref=fresh.at[pl.ds(pl.multiple_of(chunk * CHUNK, CHUNK), CHUNK)],
            send_sem=fresh_send.at[step],
            recv_sem=fresh_recv.at[step],
            device_id=target,
            device_id_type=MESH,
        )

    def back_copy(step):
        other, target = far_peer(step)
        return pltpu.make_async_remote_copy(
            src_ref=back_out.at[other],
            dst_ref=back.at[place],
            send_sem=back_send.at[step],
            recv_sem=back_recv.at[step],
            device_id=target,
            device_id_type=MESH,
        )

    def last_copy(step):
        other, target = near_peer(step)
        their_chunk = other % SLOTS
        their_slot = (their_chunk % PLAYERS) * ACTIONS + their_chunk // PLAYERS
        return pltpu.make_async_remote_copy(
            src_ref=last_out.at[(other // SLOTS) * SLOTS + their_slot],
            dst_ref=last.at[half * SLOTS + chunk],
            send_sem=last_send.at[step],
            recv_sem=last_recv.at[step],
            device_id=target,
            device_id_type=MESH,
        )

    def each(count, action_of):
        def body(step, carry):
            action_of(step)
            return carry

        lax.fori_loop(1, count, body, 0)

    barrier = pltpu.get_barrier_semaphore()

    def greet_near(step):
        other, target = near_peer(step)
        pl.semaphore_signal(barrier, inc=1, device_id=target, device_id_type=MESH)

    def greet_far(step):
        other, target = far_peer(step)
        pl.semaphore_signal(barrier, inc=1, device_id=target, device_id_type=MESH)

    each(HALVES * SLOTS, greet_near)
    each(ring, greet_far)

    own_cluster = jnp.full((1, LANES), cluster[0], jnp.int32)
    cluster_out[...] = own_cluster
    clusters[place] = own_cluster
    nodes = SLOTS * CHUNK
    line = lax.broadcasted_iota(jnp.int32, (nodes, nodes), 0)
    column = lax.broadcasted_iota(jnp.int32, (nodes, nodes), 1)
    diagonal = line == column
    pot_rows = jnp.sum(jnp.where(diagonal, pot[...], 0.0), axis=1, keepdims=True)
    code_rows = jnp.sum(
        jnp.where(diagonal, codes[...].astype(jnp.float32), 0.0), axis=1, keepdims=True
    )
    meta_out[:, :, :LANES] = jnp.broadcast_to(pot_rows, (nodes, LANES)).reshape(
        SLOTS, CHUNK, LANES
    )
    meta_out[:, :, LANES:] = jnp.broadcast_to(code_rows, (nodes, LANES)).reshape(
        SLOTS, CHUNK, LANES
    )
    pl.semaphore_wait(barrier, HALVES * SLOTS - 1 + ring - 1)

    each(HALVES * SLOTS, lambda step: near_copy(step).start())
    each(ring, lambda step: cluster_copy(step).start())
    each(SLOTS, lambda step: regret_copy(step).start())
    each(SLOTS, lambda step: meta_copy(step).start())
    keep_regret = pltpu.make_async_copy(
        regrets.at[pl.ds(pl.multiple_of(chunk * CHUNK, CHUNK), CHUNK)],
        regret.at[slot],
        local_sem.at[0],
    )
    keep_regret.start()
    near[half * SLOTS + slot] = turn[chunk]
    meta[slot] = meta_out[chunk]

    rank_row = ranks[...].astype(jnp.float32)

    def build_strength(block, carry):
        first = pl.multiple_of(block * LANES, LANES)
        mine = ranks[:, pl.ds(first, LANES)].astype(jnp.float32)
        rank_column = jnp.broadcast_to(mine, (LANES, LANES)).T
        for tile in range(width // LANES):
            span = slice(tile * LANES, (tile + 1) * LANES)
            sign = jnp.minimum(jnp.maximum(rank_row[:, span] - rank_column, -1.0), 1.0)
            strength[pl.ds(first, LANES), span] = sign.astype(jnp.bfloat16)
        return carry

    lax.fori_loop(0, width // LANES, build_strength, 0)

    each(HALVES * SLOTS, lambda step: near_copy(step).wait_recv())
    each(ring, lambda step: cluster_copy(step).wait_recv())
    low = lax.broadcasted_iota(jnp.int32, (SLOTS, CHUNK, LANES), 2) < PIECE
    parts = []
    lower = near[:SLOTS].astype(jnp.float32)
    upper = near[SLOTS:].astype(jnp.float32)
    for pair in range(CLUSTERS // 2):
        rows = slice(pair * CHUNK, (pair + 1) * CHUNK)
        first, second = lower[:, rows], upper[:, rows]
        parts.append(jnp.where(low, first, pltpu.roll(second, PIECE, 2)))
        parts.append(jnp.where(low, pltpu.roll(first, PIECE, 2), second))
    panels = [part.reshape(ROWS, LANES) for part in parts]

    def choose(step, carry):
        other = (place + step) % ring
        wanted = clusters[other]
        result = panels[0]
        for index in range(1, CLUSTERS):
            result = jnp.where(wanted == index, panels[index], result)
        far_out[other] = result.astype(jnp.bfloat16)
        return carry

    def choose_and_send(step):
        choose(step, 0)
        far_copy(step).start()

    each(ring, choose_and_send)
    choose(0, 0)
    far[:, pl.ds(pl.multiple_of(place * LANES, LANES), LANES)] = far_out[place]

    bucket = mapping[...]
    shard, within = bucket // PIECE, bucket % PIECE
    ordered = (shard % ring) * LANES + (shard // ring) * PIECE + within

    def build_onehot(block, carry):
        first = pl.multiple_of(block * LANES, LANES)
        index = lax.broadcasted_iota(jnp.int32, (LANES, LANES), 0) + first
        for tile in range(width // LANES):
            span = slice(tile * LANES, (tile + 1) * LANES)
            hit = jnp.where(ordered[:, span] == index, 1.0, 0.0)
            onehot[pl.ds(first, LANES), span] = hit.astype(jnp.bfloat16)
        return carry

    lax.fori_loop(0, depth // LANES, build_onehot, 0)

    each(SLOTS, lambda step: regret_copy(step).wait_recv())
    keep_regret.wait()
    each(SLOTS, lambda step: meta_copy(step).wait_recv())
    step_width = min(256, width)

    def match(tile, carry):
        span = pl.ds(pl.multiple_of(tile * step_width, step_width), step_width)
        for who in range(PLAYERS):
            positive = [
                jnp.maximum(regret[who * ACTIONS + act, :, span], 0.0) for act in range(ACTIONS)
            ]
            total = (positive[0] + positive[1]) + (positive[2] + positive[3])
            inverse = 1.0 / (total + ACTIONS * SMOOTH)
            for act in range(ACTIONS):
                sigma[who * ACTIONS + act, :, span] = (positive[act] + SMOOTH) * inverse
        return carry

    lax.fori_loop(0, width // step_width, match, 0)

    each(ring, lambda step: far_copy(step).wait_recv())

    def lift(tile, totals):
        span = pl.ds(pl.multiple_of(tile * step_width, step_width), step_width)
        lifted = jnp.dot(far[...], onehot[:, span], preferred_element_type=jnp.float32)
        now = (lifted * sigma[:, :, span].reshape(ROWS, step_width)).astype(jnp.bfloat16)
        reach[:, span] = now
        return totals + jnp.sum(now.astype(jnp.float32), axis=1, keepdims=True)

    totals = lax.fori_loop(0, width // step_width, lift, jnp.zeros((ROWS, 1), jnp.float32))

    def opponent(rows):
        return jnp.concatenate([rows[ROWS // 2 :], rows[: ROWS // 2]], axis=0)

    pot_here = meta[:, :, :LANES].reshape(ROWS, LANES) * scale
    code_here = meta[:, :, LANES:].reshape(ROWS, LANES)
    row = lax.broadcasted_iota(jnp.int32, (ROWS, LANES), 0)
    who_here = jnp.where(row >= ROWS // 2, 1.0, 0.0)
    signed = jnp.where(code_here == who_here, -pot_here, pot_here)
    fold = signed * opponent(totals)
    repeats = step_width // LANES
    fold_wide = jnp.concatenate([fold] * repeats, axis=1)
    pot_wide = jnp.concatenate([pot_here] * repeats, axis=1)
    show_wide = jnp.concatenate([code_here] * repeats, axis=1) == 2.0

    def evaluate(tile, carry):
        span = pl.ds(pl.multiple_of(tile * step_width, step_width), step_width)
        equity = jnp.dot(reach[...], strength[:, span], preferred_element_type=jnp.float32)
        value = jnp.where(show_wide, pot_wide * opponent(equity), fold_wide)
        value = value.reshape(PLAYERS, ACTIONS, CHUNK, step_width)
        play = sigma[:, :, span].reshape(PLAYERS, ACTIONS, CHUNK, step_width)
        share = play * value
        node = (share[:, 0] + share[:, 1]) + (share[:, 2] + share[:, 3])
        before = regret[:, :, span].reshape(PLAYERS, ACTIONS, CHUNK, step_width)
        after = (before + value) - node[:, None]
        updated[:, :, span] = after.reshape(SLOTS, CHUNK, step_width)
        weighted[:, span] = share.reshape(ROWS, step_width).astype(jnp.bfloat16)
        return carry

    lax.fori_loop(0, width // step_width, evaluate, 0)

    each(SLOTS, lambda step: fresh_copy(step).start())
    keep_fresh = pltpu.make_async_copy(
        updated.at[slot],
        fresh.at[pl.ds(pl.multiple_of(chunk * CHUNK, CHUNK), CHUNK)],
        local_sem.at[1],
    )
    keep_fresh.start()

    def project(step):
        other = (place + step) % ring
        rows = pl.ds(pl.multiple_of(other * LANES, LANES), LANES)
        block = lax.dot_general(
            weighted[...],
            onehot[rows, :],
            (((1,), (1,)), ((), ())),
            preferred_element_type=jnp.float32,
        )
        back_out[other] = block.astype(jnp.bfloat16)

    def project_and_send(step):
        project(step)
        back_copy(step).start()

    each(ring, project_and_send)
    project(0)
    back[place] = back_out[place]

    each(ring, lambda step: back_copy(step).wait_recv())
    held = [jnp.zeros((ROWS, LANES), jnp.float32) for unused in range(CLUSTERS)]
    for source in range(ring):
        block = back[source].astype(jnp.float32)
        theirs = clusters[source]
        for index in range(CLUSTERS):
            held[index] = held[index] + jnp.where(theirs == index, block, 0.0)
    held = [part.reshape(SLOTS, CHUNK, LANES) for part in held]
    for pair in range(CLUSTERS // 2):
        rows = slice(pair * CHUNK, (pair + 1) * CHUNK)
        first, second = held[2 * pair], held[2 * pair + 1]
        last_out[:SLOTS, rows] = jnp.where(low, first, pltpu.roll(second, PIECE, 2))
        last_out[SLOTS:, rows] = jnp.where(low, pltpu.roll(first, PIECE, 2), second)

    each(HALVES * SLOTS, lambda step: last_copy(step).start())
    last[half * SLOTS + chunk] = last_out[half * SLOTS + slot]
    each(HALVES * SLOTS, lambda step: last_copy(step).wait_recv())
    shares[...] = last[:SLOTS] + last[SLOTS:]

    each(SLOTS, lambda step: fresh_copy(step).wait_recv())
    keep_fresh.wait()

    def finish_same(step):
        regret_copy(step).wait_send()
        meta_copy(step).wait_send()
        fresh_copy(step).wait_send()

    def finish_near(step):
        near_copy(step).wait_send()
        last_copy(step).wait_send()

    def finish_far(step):
        cluster_copy(step).wait_send()
        far_copy(step).wait_send()
        back_copy(step).wait_send()

    each(SLOTS, finish_same)
    each(HALVES * SLOTS, finish_near)
    each(ring, finish_far)


def on_device(ring, turn_reach, regrets, pot, turn_cluster, bucket_map, codes, ranks):
    width = ranks.shape[1]
    depth = ring * LANES
    near = HALVES * SLOTS
    halves = CLUSTERS // 2
    tile = (halves * CHUNK, 2 * PIECE)
    turn = (
        turn_reach[0]
        .reshape(PIECE, halves, 2, SLOTS, CHUNK)
        .transpose(3, 1, 4, 2, 0)
        .reshape(SLOTS, *tile)
    )
    vmem = pl.BlockSpec(memory_space=pltpu.VMEM)
    dma = pltpu.SemaphoreType.DMA
    fresh, shares = pl.pallas_call(
        functools.partial(kernel, ring),
        out_shape=(
            jax.ShapeDtypeStruct((SLOTS * CHUNK, width), jnp.float32),
            jax.ShapeDtypeStruct((SLOTS, *tile), jnp.float32),
        ),
        in_specs=[
            pl.BlockSpec(memory_space=pl.ANY),
            vmem,
            vmem,
            vmem,
            pl.BlockSpec(memory_space=pltpu.SMEM),
            vmem,
            vmem,
        ],
        out_specs=(pl.BlockSpec(memory_space=pl.ANY), vmem),
        scratch_shapes=[
            pltpu.VMEM((depth, width), jnp.bfloat16),
            pltpu.VMEM((width, width), jnp.bfloat16),
            pltpu.VMEM((SLOTS, CHUNK, 2 * LANES), jnp.float32),
            pltpu.VMEM((SLOTS, CHUNK, 2 * LANES), jnp.float32),
            pltpu.VMEM((SLOTS, CHUNK, width), jnp.float32),
            pltpu.VMEM((SLOTS, CHUNK, width), jnp.float32),
            pltpu.VMEM((near, *tile), jnp.bfloat16),
            pltpu.VMEM((1, LANES), jnp.int32),
            pltpu.VMEM((ring, 1, LANES), jnp.int32),
            pltpu.VMEM((ring, ROWS, LANES), jnp.bfloat16),
            pltpu.VMEM((ROWS, depth), jnp.bfloat16),
            pltpu.VMEM((ROWS, width), jnp.bfloat16),
            pltpu.VMEM((SLOTS, CHUNK, width), jnp.float32),
            pltpu.VMEM((ROWS, width), jnp.bfloat16),
            pltpu.VMEM((ring, ROWS, LANES), jnp.bfloat16),
            pltpu.VMEM((ring, ROWS, LANES), jnp.bfloat16),
            pltpu.VMEM((near, *tile), jnp.float32),
            pltpu.VMEM((near, *tile), jnp.float32),
            dma((SLOTS,)),
            dma((SLOTS,)),
            dma((SLOTS,)),
            dma((SLOTS,)),
            dma((near,)),
            dma((near,)),
            dma((ring,)),
            dma((ring,)),
            dma((ring,)),
            dma((ring,)),
            dma((SLOTS,)),
            dma((SLOTS,)),
            dma((ring,)),
            dma((ring,)),
            dma((near,)),
            dma((near,)),
            dma((2,)),
        ],
        compiler_params=pltpu.CompilerParams(
            collective_id=0, has_side_effects=True, vmem_limit_bytes=40 * 2**20
        ),
    )(
        regrets[0, 0],
        turn,
        pot[None],
        codes[None],
        turn_cluster,
        bucket_map,
        ranks,
    )
    shares = (
        shares.reshape(SLOTS, halves, CHUNK, 2, PIECE)
        .transpose(4, 1, 3, 0, 2)
        .reshape(1, PIECE, CLUSTERS, SLOTS * CHUNK)
    )
    return fresh[None, None], shares


def solution(mesh):
    return jax.shard_map(
        functools.partial(on_device, mesh.shape["board"] // HALVES),
        mesh=mesh,
        in_specs=(
            P("pair", "board", None, "hist"),
            P("pair", "board", "hist", None),
            P("hist"),
            P("board"),
            P("board", None),
            P("hist"),
            P("board", None),
        ),
        out_specs=(P("pair", "board", "hist", None), P("pair", "board", None, "hist")),
        check_vma=False,
    )
```

```python
import functools

import jax
import jax.numpy as jnp
from jax import lax
from jax.experimental import pallas as pl
from jax.experimental.pallas import tpu as pltpu
from jax.sharding import PartitionSpec as P

ACTIONS = 4
CLUSTERS = 4
PLAYERS = 2
SMOOTH = 0.01
CHUNK = 8
SLOTS = PLAYERS * ACTIONS
ROWS = SLOTS * CHUNK
HALVES = 2
PIECE = 64
CORES = 2
LANES = 128
MESH = pl.DeviceIdType.MESH


def kernel(
    regrets,
    turn_reach,
    pot,
    codes,
    cluster,
    mapping,
    ranks,
    fresh,
    shares,
    onehot,
    spread,
    strength,
    turn_raw,
    turn_rows,
    turn,
    pot_row,
    code_row,
    map_row,
    rank_row,
    meta_out,
    meta,
    regret,
    sigma,
    near,
    cluster_out,
    clusters,
    far_out,
    far,
    lifted,
    reach,
    updated,
    weighted,
    back_out,
    back,
    last_out,
    last,
    fetch_sem,
    regret_send,
    regret_recv,
    meta_send,
    meta_recv,
    near_send,
    near_recv,
    cluster_send,
    cluster_recv,
    far_send,
    far_recv,
    fresh_send,
    fresh_recv,
    back_send,
    back_recv,
    last_send,
    last_recv,
    local_sem,
):
    width = ranks.shape[1]
    ring = far_send.shape[0]
    chips = ring // CORES
    board = lax.axis_index("board")
    action = lax.axis_index("hist")
    player = lax.axis_index("pair")
    half = board // ring
    place = board % ring
    chip = place // CORES
    core = place % CORES
    chunk = action * PLAYERS + player
    slot = player * ACTIONS + action
    group = half * SLOTS + chunk
    scale = width ** (-0.5)
    inward = [(i + 1) // 2 if i % 2 else (chips - i // 2) % chips for i in range(chips)]
    outward = inward[::-1]

    def same_board(step):
        other = (chunk + step) % SLOTS
        return other, {"board": board, "hist": other // PLAYERS, "pair": other % PLAYERS}

    def near_peer(step):
        other = (group + step) % (HALVES * SLOTS)
        their_chunk = other % SLOTS
        target = {
            "board": (other // SLOTS) * ring + place,
            "hist": their_chunk // PLAYERS,
            "pair": their_chunk % PLAYERS,
        }
        return other, target

    def far_peer(step):
        there = (chip + step // CORES) % chips
        mate = (core + step) % CORES
        other = there * CORES + mate
        target = {"board": half * ring + other, "hist": action, "pair": player}
        return there, mate, other, target

    def lanes_of(index):
        return pl.ds(pl.multiple_of(index * LANES, LANES), LANES)

    def chunk_of(index):
        return pl.ds(pl.multiple_of(index * CHUNK, CHUNK), CHUNK)

    def remote(src, dst, send, recv, step, target):
        return pltpu.make_async_remote_copy(
            src_ref=src,
            dst_ref=dst,
            send_sem=send.at[step],
            recv_sem=recv.at[step],
            device_id=target,
            device_id_type=MESH,
        )

    def regret_copy(step):
        other, target = same_board(step)
        return remote(
            regrets.at[chunk_of(other)], regret.at[slot], regret_send, regret_recv, step, target
        )

    def meta_copy(step):
        other, target = same_board(step)
        return remote(meta_out.at[other], meta.at[slot], meta_send, meta_recv, step, target)

    def near_copy(step):
        other, target = near_peer(step)
        return remote(
            turn.at[other % SLOTS],
            near.at[half * SLOTS + slot],
            near_send,
            near_recv,
            step,
            target,
        )

    def cluster_copy(step):
        there, mate, other, target = far_peer(step)
        return remote(cluster_out, clusters.at[place], cluster_send, cluster_recv, step, target)

    def far_copy(step):
        there, mate, other, target = far_peer(step)
        return remote(
            far_out.at[other], far.at[chip, :, lanes_of(core)], far_send, far_recv, step, target
        )

    def fresh_copy(step):
        other, target = same_board(step)
        their_slot = (other % PLAYERS) * ACTIONS + other // PLAYERS
        return remote(
            updated.at[their_slot],
            fresh.at[chunk_of(chunk)],
            fresh_send,
            fresh_recv,
            step,
            target,
        )

    def back_copy(step):
        there, mate, other, target = far_peer(step)
        return remote(
            back_out.at[there, :, lanes_of(mate)],
            back.at[place],
            back_send,
            back_recv,
            step,
            target,
        )

    def last_copy(step):
        other, target = near_peer(step)
        their_chunk = other % SLOTS
        their_slot = (their_chunk % PLAYERS) * ACTIONS + their_chunk // PLAYERS
        return remote(
            last_out.at[(other // SLOTS) * SLOTS + their_slot],
            last.at[half * SLOTS + chunk],
            last_send,
            last_recv,
            step,
            target,
        )

    def each(count, action_of):
        def body(step, carry):
            action_of(step)
            return carry

        lax.fori_loop(1, count, body, 0)

    fetches = [
        pltpu.make_async_copy(src, dst, fetch_sem.at[index])
        for index, (src, dst) in enumerate(
            [
                (turn_reach, turn_raw),
                (pot, pot_row),
                (codes, code_row),
                (ranks, rank_row),
                (mapping, map_row),
                (regrets.at[chunk_of(chunk)], regret.at[slot]),
            ]
        )
    ]
    for fetch in fetches:
        fetch.start()

    barrier = pltpu.get_barrier_semaphore()

    def greet_near(step):
        other, target = near_peer(step)
        pl.semaphore_signal(barrier, inc=1, device_id=target, device_id_type=MESH)

    def greet_far(step):
        there, mate, other, target = far_peer(step)
        pl.semaphore_signal(barrier, inc=1, device_id=target, device_id_type=MESH)

    each(ring, greet_far)
    each(HALVES * SLOTS, greet_near)

    own_cluster = jnp.full((1, LANES), cluster[0], jnp.int32)
    cluster_out[...] = own_cluster
    clusters[place] = own_cluster
    for fetch in fetches[:3]:
        fetch.wait()
    nodes = SLOTS * CHUNK
    turn_rows[...] = turn_raw[...].astype(jnp.float32)
    columns = []
    for pair in range(CLUSTERS // 2):
        both = jnp.concatenate([turn_rows[:, 2 * pair, :], turn_rows[:, 2 * pair + 1, :]], axis=0)
        columns.append(both.T.reshape(SLOTS, CHUNK, 2 * PIECE))
    turn[...] = jnp.concatenate(columns, axis=1).astype(jnp.bfloat16)
    line = lax.broadcasted_iota(jnp.int32, (nodes, nodes), 0)
    column = lax.broadcasted_iota(jnp.int32, (nodes, nodes), 1)
    diagonal = line == column
    pot_rows = jnp.sum(jnp.where(diagonal, pot_row[...], 0.0), axis=1, keepdims=True)
    code_rows = jnp.sum(
        jnp.where(diagonal, code_row[...].astype(jnp.float32), 0.0), axis=1, keepdims=True
    )
    meta_out[:, :, :LANES] = jnp.broadcast_to(pot_rows, (nodes, LANES)).reshape(
        SLOTS, CHUNK, LANES
    )
    meta_out[:, :, LANES:] = jnp.broadcast_to(code_rows, (nodes, LANES)).reshape(
        SLOTS, CHUNK, LANES
    )
    near[half * SLOTS + slot] = turn[chunk]
    meta[slot] = meta_out[chunk]
    pl.semaphore_wait(barrier, HALVES * SLOTS - 1 + ring - 1)

    each(HALVES * SLOTS, lambda step: near_copy(step).start())
    each(ring, lambda step: cluster_copy(step).start())
    each(SLOTS, lambda step: meta_copy(step).start())
    each(SLOTS, lambda step: regret_copy(step).start())

    for fetch in fetches[3:5]:
        fetch.wait()
    rank_wide = rank_row[...].astype(jnp.float32)

    def build_strength(block, carry):
        mine = rank_row[:, lanes_of(block)].astype(jnp.float32)
        rank_column = jnp.broadcast_to(mine, (LANES, LANES)).T
        for tile in range(width // LANES):
            span = slice(tile * LANES, (tile + 1) * LANES)
            sign = jnp.minimum(jnp.maximum(rank_wide[:, span] - rank_column, -1.0), 1.0)
            strength[lanes_of(block), span] = sign.astype(jnp.bfloat16)
        return carry

    lax.fori_loop(0, width // LANES, build_strength, 0)

    each(HALVES * SLOTS, lambda step: near_copy(step).wait_recv())
    each(ring, lambda step: cluster_copy(step).wait_recv())
    low = lax.broadcasted_iota(jnp.int32, (SLOTS, CHUNK, LANES), 2) < PIECE
    parts = []
    lower = near[:SLOTS].astype(jnp.float32)
    upper = near[SLOTS:].astype(jnp.float32)
    for pair in range(CLUSTERS // 2):
        rows = slice(pair * CHUNK, (pair + 1) * CHUNK)
        first, second = lower[:, rows], upper[:, rows]
        parts.append(jnp.where(low, first, pltpu.roll(second, PIECE, 2)))
        parts.append(jnp.where(low, pltpu.roll(first, PIECE, 2), second))
    panels = [part.reshape(ROWS, LANES) for part in parts]

    def choose(other):
        wanted = clusters[other]
        result = panels[0]
        for index in range(1, CLUSTERS):
            result = jnp.where(wanted == index, panels[index], result)
        return result.astype(jnp.bfloat16)

    for distance in outward:
        for step in range(distance * CORES, (distance + 1) * CORES):
            if step > 0:
                there, mate, other, target = far_peer(step)
                far_out[other] = choose(other)
                far_copy(step).start()
    far[chip, :, lanes_of(core)] = choose(place)

    bucket = map_row[...]
    shard, within = bucket // PIECE, bucket % PIECE
    map_row[...] = (shard % ring) * LANES + (shard // ring) * PIECE + within
    map_wide = map_row[...]
    tiles = ring * LANES // LANES

    def build_onehot(block, carry):
        index = lax.broadcasted_iota(jnp.int32, (LANES, LANES), 0) + block * LANES
        for tile in range(width // LANES):
            span = slice(tile * LANES, (tile + 1) * LANES)
            hit = jnp.where(map_wide[:, span] == index, 1.0, 0.0)
            onehot[lanes_of(block), span] = hit.astype(jnp.bfloat16)
        return carry

    lax.fori_loop(0, tiles, build_onehot, 0)

    def build_spread(block, carry):
        mine = map_row[:, lanes_of(block)].astype(jnp.float32)
        map_column = jnp.broadcast_to(mine, (LANES, LANES)).T.astype(jnp.int32)
        index = lax.broadcasted_iota(jnp.int32, (LANES, LANES), 1)
        for tile in range(tiles):
            span = slice(tile * LANES, (tile + 1) * LANES)
            hit = jnp.where(map_column == index + tile * LANES, 1.0, 0.0)
            spread[lanes_of(block), span] = hit.astype(jnp.bfloat16)
        return carry

    lax.fori_loop(0, width // LANES, build_spread, 0)

    step_width = min(512, width)
    spans = [slice(first, first + step_width) for first in range(0, width, step_width)]

    def match(span):
        for who in range(PLAYERS):
            positive = [
                jnp.maximum(regret[who * ACTIONS + act, :, span], 0.0) for act in range(ACTIONS)
            ]
            total = (positive[0] + positive[1]) + (positive[2] + positive[3])
            inverse = 1.0 / (total + ACTIONS * SMOOTH)
            for act in range(ACTIONS):
                sigma[who * ACTIONS + act, :, span] = (positive[act] + SMOOTH) * inverse

    totals = jnp.zeros((ROWS, 1), jnp.float32)
    for turn_of, distance in enumerate(inward):
        if turn_of == chips // 2:
            each(SLOTS, lambda step: regret_copy(step).wait_recv())
            fetches[5].wait()
            for span in spans:
                match(span)
        for step in range(distance * CORES, (distance + 1) * CORES):
            if step > 0:
                far_copy(step).wait_recv()
        source = (chip + chips - distance) % chips
        rows = pl.ds(pl.multiple_of(source * CORES * LANES, CORES * LANES), CORES * LANES)
        panel = far[source]
        for span in spans:
            now = jnp.dot(panel, onehot[rows, span], preferred_element_type=jnp.float32)
            if turn_of > 0:
                now = now + lifted[:, span]
            if turn_of < chips - 1:
                lifted[:, span] = now
            else:
                now = (now * sigma[:, :, span].reshape(ROWS, step_width)).astype(jnp.bfloat16)
                reach[:, span] = now
                totals = totals + jnp.sum(now.astype(jnp.float32), axis=1, keepdims=True)

    def opponent(rows):
        return jnp.concatenate([rows[ROWS // 2 :], rows[: ROWS // 2]], axis=0)

    each(SLOTS, lambda step: meta_copy(step).wait_recv())
    pot_here = meta[:, :, :LANES].reshape(ROWS, LANES) * scale
    code_here = meta[:, :, LANES:].reshape(ROWS, LANES)
    row = lax.broadcasted_iota(jnp.int32, (ROWS, LANES), 0)
    who_here = jnp.where(row >= ROWS // 2, 1.0, 0.0)
    signed = jnp.where(code_here == who_here, -pot_here, pot_here)
    fold = signed * opponent(totals)
    repeats = step_width // LANES
    fold_wide = jnp.concatenate([fold] * repeats, axis=1)
    pot_wide = jnp.concatenate([pot_here] * repeats, axis=1)
    show_wide = jnp.concatenate([code_here] * repeats, axis=1) == 2.0

    for span in spans:
        equity = jnp.dot(reach[...], strength[:, span], preferred_element_type=jnp.float32)
        value = jnp.where(show_wide, pot_wide * opponent(equity), fold_wide)
        updated[:, :, span] = value.reshape(SLOTS, CHUNK, step_width)
        share = sigma[:, :, span].reshape(ROWS, step_width) * value
        weighted[:, span] = share.astype(jnp.bfloat16)

    for distance in outward:
        there = (chip + distance) % chips
        columns_there = pl.ds(pl.multiple_of(there * CORES * LANES, CORES * LANES), CORES * LANES)
        block = jnp.dot(
            weighted[...], spread[:, columns_there], preferred_element_type=jnp.float32
        )
        back_out[there] = block.astype(jnp.bfloat16)
        for step in range(distance * CORES, (distance + 1) * CORES):
            if step > 0:
                back_copy(step).start()
    back[place] = back_out[chip, :, lanes_of(core)]

    def renew(tile, carry):
        span = lanes_of(tile)
        for who in range(PLAYERS):
            those = [who * ACTIONS + act for act in range(ACTIONS)]
            value = [updated[index, :, span] for index in those]
            share = [sigma[index, :, span] * now for index, now in zip(those, value)]
            node = (share[0] + share[1]) + (share[2] + share[3])
            for index, now in zip(those, value):
                updated[index, :, span] = (regret[index, :, span] + now) - node
        return carry

    lax.fori_loop(0, width // LANES, renew, 0)
    each(SLOTS, lambda step: fresh_copy(step).start())
    keep_fresh = pltpu.make_async_copy(updated.at[slot], fresh.at[chunk_of(chunk)], local_sem)
    keep_fresh.start()

    held = [jnp.zeros((ROWS, LANES), jnp.float32) for unused in range(CLUSTERS)]
    for distance in inward:
        for step in range(distance * CORES, (distance + 1) * CORES):
            if step > 0:
                back_copy(step).wait_recv()
            source = ((chip + chips - distance) % chips) * CORES + (core + step) % CORES
            block = back[source].astype(jnp.float32)
            theirs = clusters[source]
            for index in range(CLUSTERS):
                held[index] = held[index] + jnp.where(theirs == index, block, 0.0)
    held = [part.reshape(SLOTS, CHUNK, LANES) for part in held]
    for pair in range(CLUSTERS // 2):
        rows = slice(pair * CHUNK, (pair + 1) * CHUNK)
        first, second = held[2 * pair], held[2 * pair + 1]
        last_out[:SLOTS, rows] = jnp.where(low, first, pltpu.roll(second, PIECE, 2))
        last_out[SLOTS:, rows] = jnp.where(low, pltpu.roll(first, PIECE, 2), second)

    each(HALVES * SLOTS, lambda step: last_copy(step).start())
    last[half * SLOTS + chunk] = last_out[half * SLOTS + slot]

    def finish_far(step):
        cluster_copy(step).wait_send()
        far_copy(step).wait_send()
        back_copy(step).wait_send()

    def finish_same(step):
        regret_copy(step).wait_send()
        meta_copy(step).wait_send()
        fresh_copy(step).wait_send()
        fresh_copy(step).wait_recv()

    each(ring, finish_far)
    each(SLOTS, finish_same)
    keep_fresh.wait()
    each(HALVES * SLOTS, lambda step: near_copy(step).wait_send())

    each(HALVES * SLOTS, lambda step: last_copy(step).wait_recv())
    total = last[:SLOTS] + last[SLOTS:]
    for pair in range(CLUSTERS // 2):
        rows = slice(pair * CHUNK, (pair + 1) * CHUNK)
        both = total[:, rows].reshape(nodes, 2 * PIECE).T
        shares[:, 2 * pair, :] = both[:PIECE]
        shares[:, 2 * pair + 1, :] = both[PIECE:]
    each(HALVES * SLOTS, lambda step: last_copy(step).wait_send())


def on_device(ring, turn_reach, regrets, pot, turn_cluster, bucket_map, codes, ranks):
    width = ranks.shape[1]
    depth = ring * LANES
    near = HALVES * SLOTS
    nodes = SLOTS * CHUNK
    chips = ring // CORES
    tile = (CLUSTERS // 2 * CHUNK, 2 * PIECE)
    vmem = pl.BlockSpec(memory_space=pltpu.VMEM)
    hbm = pl.BlockSpec(memory_space=pltpu.HBM)
    dma = pltpu.SemaphoreType.DMA
    fresh, shares = pl.pallas_call(
        kernel,
        out_shape=(
            jax.ShapeDtypeStruct((nodes, width), jnp.float32),
            jax.ShapeDtypeStruct((PIECE, CLUSTERS, nodes), jnp.float32),
        ),
        in_specs=[hbm, hbm, hbm, hbm, pl.BlockSpec(memory_space=pltpu.SMEM), hbm, hbm],
        out_specs=(hbm, vmem),
        scratch_shapes=[
            pltpu.VMEM((depth, width), jnp.bfloat16),
            pltpu.VMEM((width, depth), jnp.bfloat16),
            pltpu.VMEM((width, width), jnp.bfloat16),
            pltpu.VMEM((PIECE, CLUSTERS, nodes), jnp.bfloat16),
            pltpu.VMEM((PIECE, CLUSTERS, nodes), jnp.float32),
            pltpu.VMEM((SLOTS, *tile), jnp.bfloat16),
            pltpu.VMEM((1, nodes), jnp.float32),
            pltpu.VMEM((1, nodes), jnp.int32),
            pltpu.VMEM((1, width), jnp.int32),
            pltpu.VMEM((1, width), jnp.int32),
            pltpu.VMEM((SLOTS, CHUNK, 2 * LANES), jnp.float32),
            pltpu.VMEM((SLOTS, CHUNK, 2 * LANES), jnp.float32),
            pltpu.VMEM((SLOTS, CHUNK, width), jnp.float32),
            pltpu.VMEM((SLOTS, CHUNK, width), jnp.float32),
            pltpu.VMEM((near, *tile), jnp.bfloat16),
            pltpu.VMEM((1, LANES), jnp.int32),
            pltpu.VMEM((ring, 1, LANES), jnp.int32),
            pltpu.VMEM((ring, ROWS, LANES), jnp.bfloat16),
            pltpu.VMEM((chips, ROWS, CORES * LANES), jnp.bfloat16),
            pltpu.VMEM((ROWS, width), jnp.float32),
            pltpu.VMEM((ROWS, width), jnp.bfloat16),
            pltpu.VMEM((SLOTS, CHUNK, width), jnp.float32),
            pltpu.VMEM((ROWS, width), jnp.bfloat16),
            pltpu.VMEM((chips, ROWS, CORES * LANES), jnp.bfloat16),
            pltpu.VMEM((ring, ROWS, LANES), jnp.bfloat16),
            pltpu.VMEM((near, *tile), jnp.float32),
            pltpu.VMEM((near, *tile), jnp.float32),
            dma((6,)),
            dma((SLOTS,)),
            dma((SLOTS,)),
            dma((SLOTS,)),
            dma((SLOTS,)),
            dma((near,)),
            dma((near,)),
            dma((ring,)),
            dma((ring,)),
            dma((ring,)),
            dma((ring,)),
            dma((SLOTS,)),
            dma((SLOTS,)),
            dma((ring,)),
            dma((ring,)),
            dma((near,)),
            dma((near,)),
            dma,
        ],
        compiler_params=pltpu.CompilerParams(
            collective_id=0, has_side_effects=True, vmem_limit_bytes=48 * 2**20
        ),
    )(
        regrets[0, 0],
        turn_reach[0],
        pot[None],
        codes[None],
        turn_cluster,
        bucket_map,
        ranks,
    )
    return fresh[None, None], shares[None]


def solution(mesh):
    return jax.shard_map(
        functools.partial(on_device, mesh.shape["board"] // HALVES),
        mesh=mesh,
        in_specs=(
            P("pair", "board", None, "hist"),
            P("pair", "board", "hist", None),
            P("hist"),
            P("board"),
            P("board", None),
            P("hist"),
            P("board", None),
        ),
        out_specs=(P("pair", "board", "hist", None), P("pair", "board", None, "hist")),
        check_vma=False,
    )
```

```python
import functools

import jax
import jax.numpy as jnp
from jax import lax
from jax.experimental import pallas as pl
from jax.experimental.pallas import tpu as pltpu
from jax.sharding import PartitionSpec as P

ACTIONS = 4
CLUSTERS = 4
PLAYERS = 2
SMOOTH = 0.01
CHUNK = 8
SLOTS = PLAYERS * ACTIONS
ROWS = SLOTS * CHUNK
HALVES = 2
PIECE = 64
CORES = 2
LANES = 128
MESH = pl.DeviceIdType.MESH
SMALL = jnp.float8_e4m3fn


def times(rows, matrix):
    return lax.dot_general(
        rows, matrix, (((1,), (0,)), ((), ())), preferred_element_type=jnp.float32
    )


def kernel(
    regrets,
    turn_reach,
    pot,
    codes,
    cluster,
    mapping,
    ranks,
    fresh,
    shares,
    onehot,
    spread,
    strength,
    turn_raw,
    turn_rows,
    turn,
    pot_row,
    code_row,
    map_row,
    rank_row,
    meta_out,
    meta,
    regret,
    sigma,
    near,
    cluster_out,
    clusters,
    far_out,
    far,
    lifted,
    reach,
    updated,
    weighted,
    back_out,
    back,
    last_out,
    last,
    fetch_sem,
    regret_send,
    regret_recv,
    meta_send,
    meta_recv,
    near_send,
    near_recv,
    cluster_send,
    cluster_recv,
    far_send,
    far_recv,
    fresh_send,
    fresh_recv,
    back_send,
    back_recv,
    last_send,
    last_recv,
    local_sem,
):
    width = ranks.shape[1]
    ring = far_send.shape[0]
    chips = ring // CORES
    board = lax.axis_index("board")
    action = lax.axis_index("hist")
    player = lax.axis_index("pair")
    half = board // ring
    place = board % ring
    chip = place // CORES
    core = place % CORES
    chunk = action * PLAYERS + player
    slot = player * ACTIONS + action
    group = half * SLOTS + chunk
    scale = width ** (-0.5)
    inward = [(i + 1) // 2 if i % 2 else (chips - i // 2) % chips for i in range(chips)]
    outward = inward[::-1]

    def same_board(step):
        other = (chunk + step) % SLOTS
        return other, {"board": board, "hist": other // PLAYERS, "pair": other % PLAYERS}

    def near_peer(step):
        other = (group + step) % (HALVES * SLOTS)
        their_chunk = other % SLOTS
        target = {
            "board": (other // SLOTS) * ring + place,
            "hist": their_chunk // PLAYERS,
            "pair": their_chunk % PLAYERS,
        }
        return other, target

    def far_peer(step):
        there = (chip + step // CORES) % chips
        mate = (core + step) % CORES
        other = there * CORES + mate
        target = {"board": half * ring + other, "hist": action, "pair": player}
        return there, mate, other, target

    def lanes_of(index):
        return pl.ds(pl.multiple_of(index * LANES, LANES), LANES)

    def chunk_of(index):
        return pl.ds(pl.multiple_of(index * CHUNK, CHUNK), CHUNK)

    def remote(src, dst, send, recv, step, target):
        return pltpu.make_async_remote_copy(
            src_ref=src,
            dst_ref=dst,
            send_sem=send.at[step],
            recv_sem=recv.at[step],
            device_id=target,
            device_id_type=MESH,
        )

    def regret_copy(step):
        other, target = same_board(step)
        return remote(
            regrets.at[chunk_of(other)], regret.at[slot], regret_send, regret_recv, step, target
        )

    def meta_copy(step):
        other, target = same_board(step)
        return remote(meta_out.at[other], meta.at[slot], meta_send, meta_recv, step, target)

    def near_copy(step):
        other, target = near_peer(step)
        return remote(
            turn.at[other % SLOTS],
            near.at[half * SLOTS + slot],
            near_send,
            near_recv,
            step,
            target,
        )

    def cluster_copy(step):
        there, mate, other, target = far_peer(step)
        return remote(cluster_out, clusters.at[place], cluster_send, cluster_recv, step, target)

    def far_copy(step):
        there, mate, other, target = far_peer(step)
        return remote(
            far_out.at[other], far.at[chip, :, lanes_of(core)], far_send, far_recv, step, target
        )

    def fresh_copy(step):
        other, target = same_board(step)
        their_slot = (other % PLAYERS) * ACTIONS + other // PLAYERS
        return remote(
            updated.at[their_slot],
            fresh.at[chunk_of(chunk)],
            fresh_send,
            fresh_recv,
            step,
            target,
        )

    def back_copy(step):
        there, mate, other, target = far_peer(step)
        return remote(
            back_out.at[there, :, lanes_of(mate)],
            back.at[place],
            back_send,
            back_recv,
            step,
            target,
        )

    def last_copy(step):
        other, target = near_peer(step)
        their_chunk = other % SLOTS
        their_slot = (their_chunk % PLAYERS) * ACTIONS + their_chunk // PLAYERS
        return remote(
            last_out.at[(other // SLOTS) * SLOTS + their_slot],
            last.at[half * SLOTS + chunk],
            last_send,
            last_recv,
            step,
            target,
        )

    def each(count, action_of):
        def body(step, carry):
            action_of(step)
            return carry

        lax.fori_loop(1, count, body, 0)

    fetches = [
        pltpu.make_async_copy(src, dst, fetch_sem.at[index])
        for index, (src, dst) in enumerate(
            [
                (turn_reach, turn_raw),
                (pot, pot_row),
                (codes, code_row),
                (ranks, rank_row),
                (mapping, map_row),
                (regrets.at[chunk_of(chunk)], regret.at[slot]),
            ]
        )
    ]
    for fetch in fetches:
        fetch.start()

    barrier = pltpu.get_barrier_semaphore()

    def greet_near(step):
        other, target = near_peer(step)
        pl.semaphore_signal(barrier, inc=1, device_id=target, device_id_type=MESH)

    def greet_far(step):
        there, mate, other, target = far_peer(step)
        pl.semaphore_signal(barrier, inc=1, device_id=target, device_id_type=MESH)

    each(ring, greet_far)
    each(HALVES * SLOTS, greet_near)

    own_cluster = jnp.full((1, LANES), cluster[0], jnp.int32)
    cluster_out[...] = own_cluster
    clusters[place] = own_cluster
    for fetch in fetches[:3]:
        fetch.wait()
    nodes = SLOTS * CHUNK
    turn_rows[...] = turn_raw[...].astype(jnp.float32)
    columns = []
    for pair in range(CLUSTERS // 2):
        both = jnp.concatenate([turn_rows[:, 2 * pair, :], turn_rows[:, 2 * pair + 1, :]], axis=0)
        columns.append(both.T.reshape(SLOTS, CHUNK, 2 * PIECE))
    turn[...] = jnp.concatenate(columns, axis=1).astype(jnp.bfloat16)
    line = lax.broadcasted_iota(jnp.int32, (nodes, nodes), 0)
    column = lax.broadcasted_iota(jnp.int32, (nodes, nodes), 1)
    diagonal = line == column
    pot_rows = jnp.sum(jnp.where(diagonal, pot_row[...], 0.0), axis=1, keepdims=True)
    code_rows = jnp.sum(
        jnp.where(diagonal, code_row[...].astype(jnp.float32), 0.0), axis=1, keepdims=True
    )
    meta_out[:, :, :LANES] = jnp.broadcast_to(pot_rows, (nodes, LANES)).reshape(
        SLOTS, CHUNK, LANES
    )
    meta_out[:, :, LANES:] = jnp.broadcast_to(code_rows, (nodes, LANES)).reshape(
        SLOTS, CHUNK, LANES
    )
    near[half * SLOTS + slot] = turn[chunk]
    meta[slot] = meta_out[chunk]
    pl.semaphore_wait(barrier, HALVES * SLOTS - 1 + ring - 1)

    each(HALVES * SLOTS, lambda step: near_copy(step).start())
    each(ring, lambda step: cluster_copy(step).start())
    each(SLOTS, lambda step: meta_copy(step).start())

    for fetch in fetches[3:5]:
        fetch.wait()
    rank_wide = rank_row[...].astype(jnp.float32)

    def build_strength(block, carry):
        mine = rank_row[:, lanes_of(block)].astype(jnp.float32)
        rank_column = jnp.broadcast_to(mine, (LANES, LANES)).T
        for tile in range(width // LANES):
            span = slice(tile * LANES, (tile + 1) * LANES)
            sign = jnp.minimum(jnp.maximum(rank_wide[:, span] - rank_column, -1.0), 1.0)
            strength[lanes_of(block), span] = sign.astype(SMALL)
        return carry

    lax.fori_loop(0, width // LANES, build_strength, 0)

    each(SLOTS, lambda step: regret_copy(step).start())

    each(HALVES * SLOTS, lambda step: near_copy(step).wait_recv())
    each(ring, lambda step: cluster_copy(step).wait_recv())
    low = lax.broadcasted_iota(jnp.int32, (SLOTS, CHUNK, LANES), 2) < PIECE
    parts = []
    lower = near[:SLOTS].astype(jnp.float32)
    upper = near[SLOTS:].astype(jnp.float32)
    for pair in range(CLUSTERS // 2):
        rows = slice(pair * CHUNK, (pair + 1) * CHUNK)
        first, second = lower[:, rows], upper[:, rows]
        parts.append(jnp.where(low, first, pltpu.roll(second, PIECE, 2)))
        parts.append(jnp.where(low, pltpu.roll(first, PIECE, 2), second))
    panels = [part.reshape(ROWS, LANES) for part in parts]

    def choose(other):
        wanted = clusters[other]
        result = panels[0]
        for index in range(1, CLUSTERS):
            result = jnp.where(wanted == index, panels[index], result)
        return result.astype(jnp.bfloat16)

    for distance in outward:
        for step in range(distance * CORES, (distance + 1) * CORES):
            if step > 0:
                there, mate, other, target = far_peer(step)
                far_out[other] = choose(other)
                far_copy(step).start()
    far[chip, :, lanes_of(core)] = choose(place)

    bucket = map_row[...]
    shard, within = bucket // PIECE, bucket % PIECE
    map_row[...] = (shard % ring) * LANES + (shard // ring) * PIECE + within
    map_wide = map_row[...]
    tiles = ring * LANES // LANES

    def build_onehot(block, carry):
        index = lax.broadcasted_iota(jnp.int32, (LANES, LANES), 0) + block * LANES
        for tile in range(width // LANES):
            span = slice(tile * LANES, (tile + 1) * LANES)
            hit = jnp.where(map_wide[:, span] == index, 1.0, 0.0)
            onehot[lanes_of(block), span] = hit.astype(SMALL)
        return carry

    lax.fori_loop(0, tiles, build_onehot, 0)

    def build_spread(block, carry):
        mine = map_row[:, lanes_of(block)].astype(jnp.float32)
        map_column = jnp.broadcast_to(mine, (LANES, LANES)).T.astype(jnp.int32)
        index = lax.broadcasted_iota(jnp.int32, (LANES, LANES), 1)
        for tile in range(tiles):
            span = slice(tile * LANES, (tile + 1) * LANES)
            hit = jnp.where(map_column == index + tile * LANES, 1.0, 0.0)
            spread[lanes_of(block), span] = hit.astype(SMALL)
        return carry

    lax.fori_loop(0, width // LANES, build_spread, 0)

    step_width = min(512, width)
    spans = [slice(first, first + step_width) for first in range(0, width, step_width)]

    def match(span):
        for who in range(PLAYERS):
            positive = [
                jnp.maximum(regret[who * ACTIONS + act, :, span], 0.0) for act in range(ACTIONS)
            ]
            total = (positive[0] + positive[1]) + (positive[2] + positive[3])
            inverse = 1.0 / (total + ACTIONS * SMOOTH)
            for act in range(ACTIONS):
                sigma[who * ACTIONS + act, :, span] = (positive[act] + SMOOTH) * inverse

    totals = jnp.zeros((ROWS, 1), jnp.float32)
    for turn_of, distance in enumerate([0] + outward[:-1]):
        if turn_of == chips // 2:
            each(SLOTS, lambda step: regret_copy(step).wait_recv())
            fetches[5].wait()
            for span in spans:
                match(span)
        for step in range(distance * CORES, (distance + 1) * CORES):
            if step > 0:
                far_copy(step).wait_recv()
        source = (chip + chips - distance) % chips
        rows = pl.ds(pl.multiple_of(source * CORES * LANES, CORES * LANES), CORES * LANES)
        panel = far[source]
        for span in spans:
            now = times(panel, onehot[rows, span])
            if turn_of > 0:
                now = now + lifted[:, span]
            if turn_of < chips - 1:
                lifted[:, span] = now
            else:
                now = (now * sigma[:, :, span].reshape(ROWS, step_width)).astype(jnp.bfloat16)
                reach[:, span] = now
                totals = totals + jnp.sum(now.astype(jnp.float32), axis=1, keepdims=True)

    def opponent(rows):
        return jnp.concatenate([rows[ROWS // 2 :], rows[: ROWS // 2]], axis=0)

    each(SLOTS, lambda step: meta_copy(step).wait_recv())
    pot_here = meta[:, :, :LANES].reshape(ROWS, LANES) * scale
    code_here = meta[:, :, LANES:].reshape(ROWS, LANES)
    row = lax.broadcasted_iota(jnp.int32, (ROWS, LANES), 0)
    who_here = jnp.where(row >= ROWS // 2, 1.0, 0.0)
    signed = jnp.where(code_here == who_here, -pot_here, pot_here)
    fold = signed * opponent(totals)
    repeats = step_width // LANES
    fold_wide = jnp.concatenate([fold] * repeats, axis=1)
    pot_wide = jnp.concatenate([pot_here] * repeats, axis=1)
    show_wide = jnp.concatenate([code_here] * repeats, axis=1) == 2.0

    for span in spans:
        equity = times(reach[...], strength[:, span])
        value = jnp.where(show_wide, pot_wide * opponent(equity), fold_wide)
        updated[:, :, span] = value.reshape(SLOTS, CHUNK, step_width)
        share = sigma[:, :, span].reshape(ROWS, step_width) * value
        weighted[:, span] = share.astype(jnp.bfloat16)

    def renew(tile, carry):
        span = lanes_of(tile)
        for who in range(PLAYERS):
            those = [who * ACTIONS + act for act in range(ACTIONS)]
            value = [updated[index, :, span] for index in those]
            share = [sigma[index, :, span] * now for index, now in zip(those, value)]
            node = (share[0] + share[1]) + (share[2] + share[3])
            for index, now in zip(those, value):
                updated[index, :, span] = (regret[index, :, span] + now) - node
        return carry

    keep_fresh = pltpu.make_async_copy(updated.at[slot], fresh.at[chunk_of(chunk)], local_sem)

    for turn_of, distance in enumerate(outward):
        if turn_of == chips // 2:
            lax.fori_loop(0, width // LANES, renew, 0)
            each(SLOTS, lambda step: fresh_copy(step).start())
            keep_fresh.start()
        there = (chip + distance) % chips
        columns_there = pl.ds(pl.multiple_of(there * CORES * LANES, CORES * LANES), CORES * LANES)
        block = times(weighted[...], spread[:, columns_there])
        back_out[there] = block.astype(jnp.bfloat16)
        for step in range(distance * CORES, (distance + 1) * CORES):
            if step > 0:
                back_copy(step).start()
    back[place] = back_out[chip, :, lanes_of(core)]

    held = [jnp.zeros((ROWS, LANES), jnp.float32) for unused in range(CLUSTERS)]
    for distance in inward:
        for step in range(distance * CORES, (distance + 1) * CORES):
            if step > 0:
                back_copy(step).wait_recv()
            source = ((chip + chips - distance) % chips) * CORES + (core + step) % CORES
            block = back[source].astype(jnp.float32)
            theirs = clusters[source]
            for index in range(CLUSTERS):
                held[index] = held[index] + jnp.where(theirs == index, block, 0.0)
    held = [part.reshape(SLOTS, CHUNK, LANES) for part in held]
    for pair in range(CLUSTERS // 2):
        rows = slice(pair * CHUNK, (pair + 1) * CHUNK)
        first, second = held[2 * pair], held[2 * pair + 1]
        last_out[:SLOTS, rows] = jnp.where(low, first, pltpu.roll(second, PIECE, 2))
        last_out[SLOTS:, rows] = jnp.where(low, pltpu.roll(first, PIECE, 2), second)

    each(HALVES * SLOTS, lambda step: last_copy(step).start())
    last[half * SLOTS + chunk] = last_out[half * SLOTS + slot]

    def finish_far(step):
        cluster_copy(step).wait_send()
        far_copy(step).wait_send()
        back_copy(step).wait_send()

    def finish_same(step):
        regret_copy(step).wait_send()
        meta_copy(step).wait_send()
        fresh_copy(step).wait_send()
        fresh_copy(step).wait_recv()

    each(ring, finish_far)
    each(SLOTS, finish_same)
    keep_fresh.wait()
    each(HALVES * SLOTS, lambda step: near_copy(step).wait_send())

    each(HALVES * SLOTS, lambda step: last_copy(step).wait_recv())
    total = last[:SLOTS] + last[SLOTS:]
    for pair in range(CLUSTERS // 2):
        rows = slice(pair * CHUNK, (pair + 1) * CHUNK)
        both = total[:, rows].reshape(nodes, 2 * PIECE).T
        shares[:, 2 * pair, :] = both[:PIECE]
        shares[:, 2 * pair + 1, :] = both[PIECE:]
    each(HALVES * SLOTS, lambda step: last_copy(step).wait_send())


def on_device(ring, turn_reach, regrets, pot, turn_cluster, bucket_map, codes, ranks):
    width = ranks.shape[1]
    depth = ring * LANES
    near = HALVES * SLOTS
    nodes = SLOTS * CHUNK
    chips = ring // CORES
    tile = (CLUSTERS // 2 * CHUNK, 2 * PIECE)
    vmem = pl.BlockSpec(memory_space=pltpu.VMEM)
    hbm = pl.BlockSpec(memory_space=pltpu.HBM)
    dma = pltpu.SemaphoreType.DMA
    fresh, shares = pl.pallas_call(
        kernel,
        out_shape=(
            jax.ShapeDtypeStruct((nodes, width), jnp.float32),
            jax.ShapeDtypeStruct((PIECE, CLUSTERS, nodes), jnp.float32),
        ),
        in_specs=[hbm, hbm, hbm, hbm, pl.BlockSpec(memory_space=pltpu.SMEM), hbm, hbm],
        out_specs=(hbm, vmem),
        scratch_shapes=[
            pltpu.VMEM((depth, width), SMALL),
            pltpu.VMEM((width, depth), SMALL),
            pltpu.VMEM((width, width), SMALL),
            pltpu.VMEM((PIECE, CLUSTERS, nodes), jnp.bfloat16),
            pltpu.VMEM((PIECE, CLUSTERS, nodes), jnp.float32),
            pltpu.VMEM((SLOTS, *tile), jnp.bfloat16),
            pltpu.VMEM((1, nodes), jnp.float32),
            pltpu.VMEM((1, nodes), jnp.int32),
            pltpu.VMEM((1, width), jnp.int32),
            pltpu.VMEM((1, width), jnp.int32),
            pltpu.VMEM((SLOTS, CHUNK, 2 * LANES), jnp.float32),
            pltpu.VMEM((SLOTS, CHUNK, 2 * LANES), jnp.float32),
            pltpu.VMEM((SLOTS, CHUNK, width), jnp.float32),
            pltpu.VMEM((SLOTS, CHUNK, width), jnp.float32),
            pltpu.VMEM((near, *tile), jnp.bfloat16),
            pltpu.VMEM((1, LANES), jnp.int32),
            pltpu.VMEM((ring, 1, LANES), jnp.int32),
            pltpu.VMEM((ring, ROWS, LANES), jnp.bfloat16),
            pltpu.VMEM((chips, ROWS, CORES * LANES), jnp.bfloat16),
            pltpu.VMEM((ROWS, width), jnp.float32),
            pltpu.VMEM((ROWS, width), jnp.bfloat16),
            pltpu.VMEM((SLOTS, CHUNK, width), jnp.float32),
            pltpu.VMEM((ROWS, width), jnp.bfloat16),
            pltpu.VMEM((chips, ROWS, CORES * LANES), jnp.bfloat16),
            pltpu.VMEM((ring, ROWS, LANES), jnp.bfloat16),
            pltpu.VMEM((near, *tile), jnp.float32),
            pltpu.VMEM((near, *tile), jnp.float32),
            dma((6,)),
            dma((SLOTS,)),
            dma((SLOTS,)),
            dma((SLOTS,)),
            dma((SLOTS,)),
            dma((near,)),
            dma((near,)),
            dma((ring,)),
            dma((ring,)),
            dma((ring,)),
            dma((ring,)),
            dma((SLOTS,)),
            dma((SLOTS,)),
            dma((ring,)),
            dma((ring,)),
            dma((near,)),
            dma((near,)),
            dma,
        ],
        compiler_params=pltpu.CompilerParams(
            collective_id=0, has_side_effects=True, vmem_limit_bytes=32 * 2**20
        ),
    )(
        *(
            pltpu.with_memory_space_constraint(x, pltpu.HBM)
            for x in (regrets[0, 0], turn_reach[0], pot[None], codes[None])
        ),
        turn_cluster,
        *(pltpu.with_memory_space_constraint(x, pltpu.HBM) for x in (bucket_map, ranks)),
    )
    return fresh[None, None], shares[None]


def solution(mesh):
    return jax.shard_map(
        functools.partial(on_device, mesh.shape["board"] // HALVES),
        mesh=mesh,
        in_specs=(
            P("pair", "board", None, "hist"),
            P("pair", "board", "hist", None),
            P("hist"),
            P("board"),
            P("board", None),
            P("hist"),
            P("board", None),
        ),
        out_specs=(P("pair", "board", "hist", None), P("pair", "board", None, "hist")),
        check_vma=False,
    )
```

```python
import functools

import jax
import jax.numpy as jnp
from jax import lax
from jax.experimental import pallas as pl
from jax.experimental.pallas import tpu as pltpu
from jax.sharding import PartitionSpec as P

ACTIONS = 4
CLUSTERS = 4
PLAYERS = 2
SMOOTH = 0.01
CHUNK = 8
SLOTS = PLAYERS * ACTIONS
ROWS = SLOTS * CHUNK
HALVES = 2
PIECE = 64
CORES = 2
LANES = 128
MESH = pl.DeviceIdType.MESH
SMALL = jnp.float8_e4m3fn


def times(rows, matrix):
    return lax.dot_general(
        rows, matrix, (((1,), (0,)), ((), ())), preferred_element_type=jnp.float32
    )


def kernel(
    regrets,
    turn_reach,
    pot,
    codes,
    cluster,
    mapping,
    ranks,
    fresh,
    shares,
    onehot,
    spread,
    strength,
    turn_raw,
    turn_rows,
    turn,
    pot_row,
    code_row,
    map_row,
    rank_row,
    meta_out,
    meta,
    regret,
    sigma,
    near,
    cluster_out,
    clusters,
    far_out,
    far,
    lifted,
    reach,
    updated,
    weighted,
    back_out,
    back,
    last_out,
    last,
    fetch_sem,
    regret_send,
    regret_recv,
    meta_send,
    meta_recv,
    near_send,
    near_recv,
    cluster_send,
    cluster_recv,
    far_send,
    far_recv,
    fresh_send,
    fresh_recv,
    back_send,
    back_recv,
    last_send,
    last_recv,
):
    width = ranks.shape[1]
    ring = back.shape[0]
    chips = ring // CORES
    board = lax.axis_index("board")
    action = lax.axis_index("hist")
    player = lax.axis_index("pair")
    half = board // ring
    place = board % ring
    chip = place // CORES
    core = place % CORES
    chunk = action * PLAYERS + player
    slot = player * ACTIONS + action
    scale = width ** (-0.5)
    inward = [(i + 1) // 2 if i % 2 else (chips - i // 2) % chips for i in range(chips)]
    outward = inward[::-1]

    def same_board(step):
        other = (chunk + step) % SLOTS
        return other, {"board": board, "hist": other // PLAYERS, "pair": other % PLAYERS}

    def near_peer(step):
        their_half = (half + step // SLOTS) % HALVES
        their_action = (action + step % SLOTS // PLAYERS) % ACTIONS
        their_player = (player + step) % PLAYERS
        their_chunk = their_action * PLAYERS + their_player
        their_slot = their_player * ACTIONS + their_action
        target = {
            "board": their_half * ring + place,
            "hist": their_action,
            "pair": their_player,
        }
        return their_half, their_chunk, their_slot, target

    def hops(step):
        along = step % SLOTS // PLAYERS
        across = 1 if step % PLAYERS else 2 * (step // SLOTS)
        return min(along, ACTIONS - along) + across

    near_steps = sorted(range(1, HALVES * SLOTS), key=hops, reverse=True)
    far_steps = [
        step
        for distance in outward
        for step in range(distance * CORES, (distance + 1) * CORES)
        if step > 0
    ]

    def far_peer(step):
        there = (chip + step // CORES) % chips
        mate = (core + step) % CORES
        other = there * CORES + mate
        target = {"board": half * ring + other, "hist": action, "pair": player}
        return there, mate, other, target

    def lanes_of(index):
        return pl.ds(pl.multiple_of(index * LANES, LANES), LANES)

    def chunk_of(index):
        return pl.ds(pl.multiple_of(index * CHUNK, CHUNK), CHUNK)

    def remote(src, dst, send, recv, target):
        return pltpu.make_async_remote_copy(
            src_ref=src,
            dst_ref=dst,
            send_sem=send,
            recv_sem=recv,
            device_id=target,
            device_id_type=MESH,
        )

    def await_bytes(buffer, semaphore):
        pltpu.make_async_copy(buffer, buffer, semaphore).wait()

    def regret_copy(step):
        other, target = same_board(step)
        return remote(
            regrets.at[chunk_of(other)], regret.at[slot], regret_send, regret_recv, target
        )

    def meta_copy(step):
        other, target = same_board(step)
        return remote(meta_out.at[other], meta.at[slot], meta_send, meta_recv, target)

    def near_copy(step):
        their_half, their_chunk, their_slot, target = near_peer(step)
        return remote(
            turn.at[their_chunk],
            near.at[half * SLOTS + slot],
            near_send,
            near_recv,
            target,
        )

    def cluster_copy(step):
        there, mate, other, target = far_peer(step)
        return remote(cluster_out, clusters.at[place], cluster_send, cluster_recv, target)

    def far_copy(step):
        there, mate, other, target = far_peer(step)
        return remote(
            far_out.at[other],
            far.at[chip, :, lanes_of(core)],
            far_send,
            far_recv.at[step // CORES],
            target,
        )

    def fresh_copy(step):
        other, target = same_board(step)
        their_slot = (other % PLAYERS) * ACTIONS + other // PLAYERS
        return remote(
            updated.at[their_slot],
            fresh.at[chunk_of(chunk)],
            fresh_send,
            fresh_recv,
            target,
        )

    def back_copy(step):
        there, mate, other, target = far_peer(step)
        return remote(
            back_out.at[there, :, lanes_of(mate)],
            back.at[place],
            back_send,
            back_recv,
            target,
        )

    def last_copy(step):
        their_half, their_chunk, their_slot, target = near_peer(step)
        return remote(
            last_out.at[their_half * SLOTS + their_slot],
            last.at[half * SLOTS + chunk],
            last_send,
            last_recv,
            target,
        )

    def each(count, action_of):
        def body(step, carry):
            action_of(step)
            return carry

        lax.fori_loop(1, count, body, 0)

    sources = [
        (turn_reach, turn_raw, fetch_sem.at[0]),
        (pot, pot_row, fetch_sem.at[1]),
        (codes, code_row, fetch_sem.at[2]),
        (ranks, rank_row, fetch_sem.at[3]),
        (mapping, map_row, fetch_sem.at[4]),
        (regrets.at[chunk_of(chunk)], regret.at[slot], regret_recv),
    ]
    fetches = [pltpu.make_async_copy(*source) for source in sources]
    fetches[0].start()

    barrier = pltpu.get_barrier_semaphore()

    def greet_near(step):
        target = near_peer(step)[-1]
        pl.semaphore_signal(barrier, inc=1, device_id=target, device_id_type=MESH)

    def greet_far(step):
        target = far_peer(step)[-1]
        pl.semaphore_signal(barrier, inc=1, device_id=target, device_id_type=MESH)

    for step in near_steps:
        greet_near(step)
    for step in far_steps:
        greet_far(step)
    for fetch in fetches[1:]:
        fetch.start()

    own_cluster = jnp.full((1, LANES), cluster[0], jnp.int32)
    cluster_out[...] = own_cluster
    clusters[place] = own_cluster
    for fetch in fetches[:3]:
        fetch.wait()
    nodes = SLOTS * CHUNK
    turn_rows[...] = turn_raw[...].astype(jnp.float32)
    columns = []
    for pair in range(CLUSTERS // 2):
        both = jnp.concatenate([turn_rows[:, 2 * pair, :], turn_rows[:, 2 * pair + 1, :]], axis=0)
        columns.append(both.T.reshape(SLOTS, CHUNK, 2 * PIECE))
    turn[...] = jnp.concatenate(columns, axis=1).astype(jnp.bfloat16)
    line = lax.broadcasted_iota(jnp.int32, (nodes, nodes), 0)
    column = lax.broadcasted_iota(jnp.int32, (nodes, nodes), 1)
    diagonal = line == column
    pot_rows = jnp.sum(jnp.where(diagonal, pot_row[...], 0.0), axis=1, keepdims=True)
    code_rows = jnp.sum(
        jnp.where(diagonal, code_row[...].astype(jnp.float32), 0.0), axis=1, keepdims=True
    )
    meta_out[:, :, :LANES] = jnp.broadcast_to(pot_rows, (nodes, LANES)).reshape(
        SLOTS, CHUNK, LANES
    )
    meta_out[:, :, LANES:] = jnp.broadcast_to(code_rows, (nodes, LANES)).reshape(
        SLOTS, CHUNK, LANES
    )
    near[half * SLOTS + slot] = turn[chunk]
    meta[slot] = meta_out[chunk]
    pl.semaphore_wait(barrier, HALVES * SLOTS - 1 + ring - 1)

    for step in near_steps:
        near_copy(step).start()
    for step in far_steps:
        cluster_copy(step).start()
    each(SLOTS, lambda step: meta_copy(step).start())

    for fetch in fetches[3:5]:
        fetch.wait()
    rank_wide = rank_row[...].astype(jnp.float32)

    def build_strength(block, carry):
        mine = rank_row[:, lanes_of(block)].astype(jnp.float32)
        rank_column = jnp.broadcast_to(mine, (LANES, LANES)).T
        for tile in range(width // LANES):
            span = slice(tile * LANES, (tile + 1) * LANES)
            sign = jnp.minimum(jnp.maximum(rank_wide[:, span] - rank_column, -1.0), 1.0)
            strength[lanes_of(block), span] = sign.astype(SMALL)
        return carry

    lax.fori_loop(0, width // LANES, build_strength, 0)

    each(SLOTS, lambda step: regret_copy(step).start())

    await_bytes(near.at[pl.ds(1, HALVES * SLOTS - 1)], near_recv)
    await_bytes(clusters.at[pl.ds(1, ring - 1)], cluster_recv)
    low = lax.broadcasted_iota(jnp.int32, (SLOTS, CHUNK, LANES), 2) < PIECE
    parts = []
    lower = near[:SLOTS].astype(jnp.float32)
    upper = near[SLOTS:].astype(jnp.float32)
    for pair in range(CLUSTERS // 2):
        rows = slice(pair * CHUNK, (pair + 1) * CHUNK)
        first, second = lower[:, rows], upper[:, rows]
        parts.append(jnp.where(low, first, pltpu.roll(second, PIECE, 2)))
        parts.append(jnp.where(low, pltpu.roll(first, PIECE, 2), second))
    panels = [part.reshape(ROWS, LANES) for part in parts]

    def choose(other):
        wanted = clusters[other]
        result = panels[0]
        for index in range(1, CLUSTERS):
            result = jnp.where(wanted == index, panels[index], result)
        return result.astype(jnp.bfloat16)

    for step in far_steps:
        other = far_peer(step)[2]
        far_out[other] = choose(other)
        far_copy(step).start()
    far[chip, :, lanes_of(core)] = choose(place)

    bucket = map_row[...]
    shard, within = bucket // PIECE, bucket % PIECE
    map_row[...] = (shard % ring) * LANES + (shard // ring) * PIECE + within
    map_wide = map_row[...]
    tiles = ring * LANES // LANES

    def build_onehot(block, carry):
        index = lax.broadcasted_iota(jnp.int32, (LANES, LANES), 0) + block * LANES
        for tile in range(width // LANES):
            span = slice(tile * LANES, (tile + 1) * LANES)
            hit = jnp.where(map_wide[:, span] == index, 1.0, 0.0)
            onehot[lanes_of(block), span] = hit.astype(SMALL)
        return carry

    lax.fori_loop(0, tiles, build_onehot, 0)

    def build_spread(block, carry):
        mine = map_row[:, lanes_of(block)].astype(jnp.float32)
        map_column = jnp.broadcast_to(mine, (LANES, LANES)).T.astype(jnp.int32)
        index = lax.broadcasted_iota(jnp.int32, (LANES, LANES), 1)
        for tile in range(tiles):
            span = slice(tile * LANES, (tile + 1) * LANES)
            hit = jnp.where(map_column == index + tile * LANES, 1.0, 0.0)
            spread[lanes_of(block), span] = hit.astype(SMALL)
        return carry

    lax.fori_loop(0, width // LANES, build_spread, 0)

    step_width = min(512, width)
    spans = [slice(first, first + step_width) for first in range(0, width, step_width)]

    def match(span):
        for who in range(PLAYERS):
            positive = [
                jnp.maximum(regret[who * ACTIONS + act, :, span], 0.0) for act in range(ACTIONS)
            ]
            total = (positive[0] + positive[1]) + (positive[2] + positive[3])
            inverse = 1.0 / (total + ACTIONS * SMOOTH)
            for act in range(ACTIONS):
                sigma[who * ACTIONS + act, :, span] = (positive[act] + SMOOTH) * inverse

    totals = jnp.zeros((ROWS, 1), jnp.float32)
    for turn_of, distance in enumerate([0] + outward[:-1]):
        if turn_of == chips // 2:
            await_bytes(regret, regret_recv)
            for span in spans:
                match(span)
        arrived = far.at[0, :, pl.ds(0, LANES)] if distance == 0 else far.at[0]
        await_bytes(arrived, far_recv.at[distance])
        source = (chip + chips - distance) % chips
        rows = pl.ds(pl.multiple_of(source * CORES * LANES, CORES * LANES), CORES * LANES)
        panel = far[source]
        for span in spans:
            now = times(panel, onehot[rows, span])
            if turn_of > 0:
                now = now + lifted[:, span]
            if turn_of < chips - 1:
                lifted[:, span] = now
            else:
                now = (now * sigma[:, :, span].reshape(ROWS, step_width)).astype(jnp.bfloat16)
                reach[:, span] = now
                totals = totals + jnp.sum(now.astype(jnp.float32), axis=1, keepdims=True)

    def opponent(rows):
        return jnp.concatenate([rows[ROWS // 2 :], rows[: ROWS // 2]], axis=0)

    await_bytes(meta.at[pl.ds(1, SLOTS - 1)], meta_recv)
    pot_here = meta[:, :, :LANES].reshape(ROWS, LANES) * scale
    code_here = meta[:, :, LANES:].reshape(ROWS, LANES)
    row = lax.broadcasted_iota(jnp.int32, (ROWS, LANES), 0)
    who_here = jnp.where(row >= ROWS // 2, 1.0, 0.0)
    signed = jnp.where(code_here == who_here, -pot_here, pot_here)
    fold = signed * opponent(totals)
    repeats = step_width // LANES
    fold_wide = jnp.concatenate([fold] * repeats, axis=1)
    pot_wide = jnp.concatenate([pot_here] * repeats, axis=1)
    show_wide = jnp.concatenate([code_here] * repeats, axis=1) == 2.0

    for span in spans:
        equity = times(reach[...], strength[:, span])
        value = jnp.where(show_wide, pot_wide * opponent(equity), fold_wide)
        updated[:, :, span] = value.reshape(SLOTS, CHUNK, step_width)
        share = sigma[:, :, span].reshape(ROWS, step_width) * value
        weighted[:, span] = share.astype(jnp.bfloat16)

    def renew(tile, carry):
        span = lanes_of(tile)
        for who in range(PLAYERS):
            those = [who * ACTIONS + act for act in range(ACTIONS)]
            value = [updated[index, :, span] for index in those]
            share = [sigma[index, :, span] * now for index, now in zip(those, value)]
            node = (share[0] + share[1]) + (share[2] + share[3])
            for index, now in zip(those, value):
                updated[index, :, span] = (regret[index, :, span] + now) - node
        return carry

    keep_fresh = pltpu.make_async_copy(updated.at[slot], fresh.at[chunk_of(chunk)], fresh_recv)

    for turn_of, distance in enumerate(outward):
        if turn_of == chips // 2:
            lax.fori_loop(0, width // LANES, renew, 0)
            each(SLOTS, lambda step: fresh_copy(step).start())
            keep_fresh.start()
        there = (chip + distance) % chips
        columns_there = pl.ds(pl.multiple_of(there * CORES * LANES, CORES * LANES), CORES * LANES)
        block = times(weighted[...], spread[:, columns_there])
        back_out[there] = block.astype(jnp.bfloat16)
        for step in range(distance * CORES, (distance + 1) * CORES):
            if step > 0:
                back_copy(step).start()
    back[place] = back_out[chip, :, lanes_of(core)]

    held = [jnp.zeros((ROWS, LANES), jnp.float32) for unused in range(CLUSTERS)]
    await_bytes(back.at[pl.ds(1, ring - 1)], back_recv)
    for source in range(ring):
        block = back[source].astype(jnp.float32)
        theirs = clusters[source]
        for index in range(CLUSTERS):
            held[index] = held[index] + jnp.where(theirs == index, block, 0.0)
    held = [part.reshape(SLOTS, CHUNK, LANES) for part in held]
    for pair in range(CLUSTERS // 2):
        rows = slice(pair * CHUNK, (pair + 1) * CHUNK)
        first, second = held[2 * pair], held[2 * pair + 1]
        last_out[:SLOTS, rows] = jnp.where(low, first, pltpu.roll(second, PIECE, 2))
        last_out[SLOTS:, rows] = jnp.where(low, pltpu.roll(first, PIECE, 2), second)

    for step in near_steps:
        last_copy(step).start()
    last[half * SLOTS + chunk] = last_out[half * SLOTS + slot]

    await_bytes(clusters.at[pl.ds(1, ring - 1)], cluster_send)
    await_bytes(far_out.at[pl.ds(1, ring - 1)], far_send)
    await_bytes(back.at[pl.ds(1, ring - 1)], back_send)
    await_bytes(regret.at[pl.ds(1, SLOTS - 1)], regret_send)
    await_bytes(meta.at[pl.ds(1, SLOTS - 1)], meta_send)
    await_bytes(near.at[pl.ds(1, HALVES * SLOTS - 1)], near_send)
    await_bytes(updated.at[pl.ds(1, SLOTS - 1)], fresh_send)
    await_bytes(updated, fresh_recv)

    await_bytes(last.at[pl.ds(1, HALVES * SLOTS - 1)], last_recv)
    total = last[:SLOTS] + last[SLOTS:]
    for pair in range(CLUSTERS // 2):
        rows = slice(pair * CHUNK, (pair + 1) * CHUNK)
        both = total[:, rows].reshape(nodes, 2 * PIECE).T
        shares[:, 2 * pair, :] = both[:PIECE]
        shares[:, 2 * pair + 1, :] = both[PIECE:]
    await_bytes(last.at[pl.ds(1, HALVES * SLOTS - 1)], last_send)


def on_device(ring, turn_reach, regrets, pot, turn_cluster, bucket_map, codes, ranks):
    width = ranks.shape[1]
    depth = ring * LANES
    near = HALVES * SLOTS
    nodes = SLOTS * CHUNK
    chips = ring // CORES
    tile = (CLUSTERS // 2 * CHUNK, 2 * PIECE)
    vmem = pl.BlockSpec(memory_space=pltpu.VMEM)
    hbm = pl.BlockSpec(memory_space=pltpu.HBM)
    dma = pltpu.SemaphoreType.DMA
    fresh, shares = pl.pallas_call(
        kernel,
        out_shape=(
            jax.ShapeDtypeStruct((nodes, width), jnp.float32),
            jax.ShapeDtypeStruct((PIECE, CLUSTERS, nodes), jnp.float32),
        ),
        in_specs=[hbm, hbm, hbm, hbm, pl.BlockSpec(memory_space=pltpu.SMEM), hbm, hbm],
        out_specs=(hbm, vmem),
        scratch_shapes=[
            pltpu.VMEM((depth, width), SMALL),
            pltpu.VMEM((width, depth), SMALL),
            pltpu.VMEM((width, width), SMALL),
            pltpu.VMEM((PIECE, CLUSTERS, nodes), jnp.bfloat16),
            pltpu.VMEM((PIECE, CLUSTERS, nodes), jnp.float32),
            pltpu.VMEM((SLOTS, *tile), jnp.bfloat16),
            pltpu.VMEM((1, nodes), jnp.float32),
            pltpu.VMEM((1, nodes), jnp.int32),
            pltpu.VMEM((1, width), jnp.int32),
            pltpu.VMEM((1, width), jnp.int32),
            pltpu.VMEM((SLOTS, CHUNK, 2 * LANES), jnp.float32),
            pltpu.VMEM((SLOTS, CHUNK, 2 * LANES), jnp.float32),
            pltpu.VMEM((SLOTS, CHUNK, width), jnp.float32),
            pltpu.VMEM((SLOTS, CHUNK, width), jnp.float32),
            pltpu.VMEM((near, *tile), jnp.bfloat16),
            pltpu.VMEM((1, LANES), jnp.int32),
            pltpu.VMEM((ring, 1, LANES), jnp.int32),
            pltpu.VMEM((ring, ROWS, LANES), jnp.bfloat16),
            pltpu.VMEM((chips, ROWS, CORES * LANES), jnp.bfloat16),
            pltpu.VMEM((ROWS, width), jnp.float32),
            pltpu.VMEM((ROWS, width), jnp.bfloat16),
            pltpu.VMEM((SLOTS, CHUNK, width), jnp.float32),
            pltpu.VMEM((ROWS, width), jnp.bfloat16),
            pltpu.VMEM((chips, ROWS, CORES * LANES), jnp.bfloat16),
            pltpu.VMEM((ring, ROWS, LANES), jnp.bfloat16),
            pltpu.VMEM((near, *tile), jnp.float32),
            pltpu.VMEM((near, *tile), jnp.float32),
            dma((5,)),
            dma,
            dma,
            dma,
            dma,
            dma,
            dma,
            dma,
            dma,
            dma,
            dma((chips,)),
            dma,
            dma,
            dma,
            dma,
            dma,
            dma,
        ],
        compiler_params=pltpu.CompilerParams(
            collective_id=0, has_side_effects=True, vmem_limit_bytes=32 * 2**20
        ),
    )(
        *(
            pltpu.with_memory_space_constraint(x, pltpu.HBM)
            for x in (regrets[0, 0], turn_reach[0], pot[None], codes[None])
        ),
        turn_cluster,
        *(pltpu.with_memory_space_constraint(x, pltpu.HBM) for x in (bucket_map, ranks)),
    )
    return fresh[None, None], shares[None]


def solution(mesh):
    return jax.shard_map(
        functools.partial(on_device, mesh.shape["board"] // HALVES),
        mesh=mesh,
        in_specs=(
            P("pair", "board", None, "hist"),
            P("pair", "board", "hist", None),
            P("hist"),
            P("board"),
            P("board", None),
            P("hist"),
            P("board", None),
        ),
        out_specs=(P("pair", "board", "hist", None), P("pair", "board", None, "hist")),
        check_vma=False,
    )
```

```python
import functools

import jax
import jax.numpy as jnp
from jax import lax
from jax.experimental import pallas as pl
from jax.experimental.pallas import tpu as pltpu
from jax.sharding import PartitionSpec as P

ACTIONS = 4
CLUSTERS = 4
PLAYERS = 2
SMOOTH = 0.01
CHUNK = 8
SLOTS = PLAYERS * ACTIONS
ROWS = SLOTS * CHUNK
HALVES = 2
PIECE = 64
CORES = 2
LANES = 128
MESH = pl.DeviceIdType.MESH
SMALL = jnp.float8_e4m3fn


def times(rows, matrix):
    return lax.dot_general(
        rows, matrix, (((1,), (0,)), ((), ())), preferred_element_type=jnp.float32
    )


def kernel(
    regrets,
    turn_reach,
    pot,
    codes,
    cluster,
    mapping,
    ranks,
    fresh,
    shares,
    onehot,
    spread,
    strength,
    turn_raw,
    turn_rows,
    turn,
    pot_row,
    code_row,
    map_row,
    rank_row,
    meta_out,
    meta,
    regret,
    sigma,
    near,
    cluster_out,
    clusters,
    far_out,
    far,
    lifted,
    reach,
    updated,
    weighted,
    back_out,
    back,
    last_out,
    last,
    fetch_sem,
    regret_send,
    regret_recv,
    meta_send,
    meta_recv,
    near_send,
    near_recv,
    cluster_send,
    cluster_recv,
    far_send,
    far_recv,
    fresh_send,
    fresh_recv,
    back_send,
    back_recv,
    last_send,
    last_recv,
):
    width = ranks.shape[1]
    ring = back.shape[0]
    chips = ring // CORES
    board = lax.axis_index("board")
    action = lax.axis_index("hist")
    player = lax.axis_index("pair")
    half = board // ring
    place = board % ring
    chip = place // CORES
    core = place % CORES
    chunk = action * PLAYERS + player
    slot = player * ACTIONS + action
    scale = width ** (-0.5)
    inward = [(i + 1) // 2 if i % 2 else (chips - i // 2) % chips for i in range(chips)]
    outward = inward[::-1]

    def same_board(step):
        other = (chunk + step) % SLOTS
        return other, {"board": board, "hist": other // PLAYERS, "pair": other % PLAYERS}

    def near_peer(step):
        their_half = (half + step // SLOTS) % HALVES
        their_action = (action + step % SLOTS // PLAYERS) % ACTIONS
        their_player = (player + step) % PLAYERS
        their_chunk = their_action * PLAYERS + their_player
        their_slot = their_player * ACTIONS + their_action
        target = {
            "board": their_half * ring + place,
            "hist": their_action,
            "pair": their_player,
        }
        return their_half, their_chunk, their_slot, target

    def hops(step):
        along = step % SLOTS // PLAYERS
        across = 1 if step % PLAYERS else 2 * (step // SLOTS)
        return min(along, ACTIONS - along) + across

    near_steps = sorted(range(1, HALVES * SLOTS), key=hops, reverse=True)
    far_steps = [
        step
        for distance in outward
        for step in range(distance * CORES, (distance + 1) * CORES)
        if step > 0
    ]

    def far_peer(step):
        there = (chip + step // CORES) % chips
        mate = (core + step) % CORES
        other = there * CORES + mate
        target = {"board": half * ring + other, "hist": action, "pair": player}
        return there, mate, other, target

    def lanes_of(index):
        return pl.ds(pl.multiple_of(index * LANES, LANES), LANES)

    def chunk_of(index):
        return pl.ds(pl.multiple_of(index * CHUNK, CHUNK), CHUNK)

    def remote(src, dst, send, recv, target):
        return pltpu.make_async_remote_copy(
            src_ref=src,
            dst_ref=dst,
            send_sem=send,
            recv_sem=recv,
            device_id=target,
            device_id_type=MESH,
        )

    def await_bytes(buffer, semaphore):
        pltpu.make_async_copy(buffer, buffer, semaphore).wait()

    def regret_copy(step):
        other, target = same_board(step)
        return remote(
            regrets.at[chunk_of(other)], regret.at[slot], regret_send, regret_recv, target
        )

    def meta_copy(step):
        other, target = same_board(step)
        return remote(meta_out.at[other], meta.at[slot], meta_send, meta_recv, target)

    def near_copy(step):
        their_half, their_chunk, their_slot, target = near_peer(step)
        return remote(
            turn.at[their_chunk],
            near.at[half * SLOTS + slot],
            near_send,
            near_recv,
            target,
        )

    def cluster_copy(step):
        there, mate, other, target = far_peer(step)
        return remote(cluster_out, clusters.at[place], cluster_send, cluster_recv, target)

    def far_copy(step):
        there, mate, other, target = far_peer(step)
        return remote(
            far_out.at[other],
            far.at[chip, :, lanes_of(core)],
            far_send,
            far_recv.at[step // CORES],
            target,
        )

    def fresh_copy(step):
        other, target = same_board(step)
        their_slot = (other % PLAYERS) * ACTIONS + other // PLAYERS
        return remote(
            updated.at[their_slot],
            fresh.at[chunk_of(chunk)],
            fresh_send,
            fresh_recv,
            target,
        )

    def back_copy(there, mate):
        target = {"board": half * ring + there * CORES + mate, "hist": action, "pair": player}
        return remote(
            back_out.at[there, :, lanes_of(mate)],
            back.at[place],
            back_send,
            back_recv,
            target,
        )

    def last_copy(there):
        their_half, rest = there // SLOTS, there % SLOTS
        their_action, their_player = rest // PLAYERS, rest % PLAYERS
        their_slot = their_player * ACTIONS + their_action
        target = {
            "board": their_half * ring + place,
            "hist": their_action,
            "pair": their_player,
        }
        return remote(
            last_out.at[their_half * SLOTS + their_slot],
            last.at[half * SLOTS + chunk],
            last_send,
            last_recv,
            target,
        )

    def each(count, action_of):
        def body(step, carry):
            action_of(step)
            return carry

        lax.fori_loop(1, count, body, 0)

    sources = [
        (turn_reach, turn_raw, fetch_sem.at[0]),
        (pot, pot_row, fetch_sem.at[1]),
        (codes, code_row, fetch_sem.at[2]),
        (ranks, rank_row, fetch_sem.at[3]),
        (mapping, map_row, fetch_sem.at[4]),
        (regrets.at[chunk_of(chunk)], regret.at[slot], regret_recv),
    ]
    fetches = [pltpu.make_async_copy(*source) for source in sources]
    fetches[0].start()

    barrier = pltpu.get_barrier_semaphore()

    def greet_near(step):
        target = near_peer(step)[-1]
        pl.semaphore_signal(barrier, inc=1, device_id=target, device_id_type=MESH)

    def greet_far(step):
        target = far_peer(step)[-1]
        pl.semaphore_signal(barrier, inc=1, device_id=target, device_id_type=MESH)

    for step in near_steps:
        greet_near(step)
    for step in far_steps:
        greet_far(step)
    for fetch in fetches[1:]:
        fetch.start()

    own_cluster = jnp.full((1, LANES), cluster[0], jnp.int32)
    cluster_out[...] = own_cluster
    clusters[place] = own_cluster
    for fetch in fetches[:3]:
        fetch.wait()
    nodes = SLOTS * CHUNK
    turn_rows[...] = turn_raw[...].astype(jnp.float32)
    columns = []
    for pair in range(CLUSTERS // 2):
        both = jnp.concatenate([turn_rows[:, 2 * pair, :], turn_rows[:, 2 * pair + 1, :]], axis=0)
        columns.append(both.T.reshape(SLOTS, CHUNK, 2 * PIECE))
    turn[...] = jnp.concatenate(columns, axis=1).astype(jnp.bfloat16)
    line = lax.broadcasted_iota(jnp.int32, (nodes, nodes), 0)
    column = lax.broadcasted_iota(jnp.int32, (nodes, nodes), 1)
    diagonal = line == column
    pot_rows = jnp.sum(jnp.where(diagonal, pot_row[...], 0.0), axis=1, keepdims=True)
    code_rows = jnp.sum(
        jnp.where(diagonal, code_row[...].astype(jnp.float32), 0.0), axis=1, keepdims=True
    )
    meta_out[:, :, :LANES] = jnp.broadcast_to(pot_rows, (nodes, LANES)).reshape(
        SLOTS, CHUNK, LANES
    )
    meta_out[:, :, LANES:] = jnp.broadcast_to(code_rows, (nodes, LANES)).reshape(
        SLOTS, CHUNK, LANES
    )
    near[half * SLOTS + slot] = turn[chunk]
    meta[slot] = meta_out[chunk]
    pl.semaphore_wait(barrier, HALVES * SLOTS - 1 + ring - 1)

    for step in near_steps:
        near_copy(step).start()
    for step in far_steps:
        cluster_copy(step).start()
    each(SLOTS, lambda step: meta_copy(step).start())

    for fetch in fetches[3:5]:
        fetch.wait()
    rank_wide = rank_row[...].astype(jnp.float32)

    def build_strength(block, carry):
        mine = rank_row[:, lanes_of(block)].astype(jnp.float32)
        rank_column = jnp.broadcast_to(mine, (LANES, LANES)).T
        for tile in range(width // LANES):
            span = slice(tile * LANES, (tile + 1) * LANES)
            sign = jnp.minimum(jnp.maximum(rank_wide[:, span] - rank_column, -1.0), 1.0)
            strength[lanes_of(block), span] = sign.astype(SMALL)
        return carry

    lax.fori_loop(0, width // LANES, build_strength, 0)

    each(SLOTS, lambda step: regret_copy(step).start())

    await_bytes(near.at[pl.ds(1, HALVES * SLOTS - 1)], near_recv)
    await_bytes(clusters.at[pl.ds(1, ring - 1)], cluster_recv)
    low = lax.broadcasted_iota(jnp.int32, (SLOTS, CHUNK, LANES), 2) < PIECE
    parts = []
    lower = near[:SLOTS].astype(jnp.float32)
    upper = near[SLOTS:].astype(jnp.float32)
    for pair in range(CLUSTERS // 2):
        rows = slice(pair * CHUNK, (pair + 1) * CHUNK)
        first, second = lower[:, rows], upper[:, rows]
        parts.append(jnp.where(low, first, pltpu.roll(second, PIECE, 2)))
        parts.append(jnp.where(low, pltpu.roll(first, PIECE, 2), second))
    panels = [part.reshape(ROWS, LANES) for part in parts]

    def choose(other):
        wanted = clusters[other]
        result = panels[0]
        for index in range(1, CLUSTERS):
            result = jnp.where(wanted == index, panels[index], result)
        return result.astype(jnp.bfloat16)

    for step in far_steps:
        other = far_peer(step)[2]
        far_out[other] = choose(other)
        far_copy(step).start()
    far[chip, :, lanes_of(core)] = choose(place)

    bucket = map_row[...]
    shard, within = bucket // PIECE, bucket % PIECE
    map_row[...] = (shard % ring) * LANES + (shard // ring) * PIECE + within
    map_wide = map_row[...]
    tiles = ring * LANES // LANES

    def build_onehot(block, carry):
        index = lax.broadcasted_iota(jnp.int32, (LANES, LANES), 0) + block * LANES
        for tile in range(width // LANES):
            span = slice(tile * LANES, (tile + 1) * LANES)
            hit = jnp.where(map_wide[:, span] == index, 1.0, 0.0)
            onehot[lanes_of(block), span] = hit.astype(SMALL)
        return carry

    lax.fori_loop(0, tiles, build_onehot, 0)

    def build_spread(block, carry):
        mine = map_row[:, lanes_of(block)].astype(jnp.float32)
        map_column = jnp.broadcast_to(mine, (LANES, LANES)).T.astype(jnp.int32)
        index = lax.broadcasted_iota(jnp.int32, (LANES, LANES), 1)
        for tile in range(tiles):
            span = slice(tile * LANES, (tile + 1) * LANES)
            hit = jnp.where(map_column == index + tile * LANES, 1.0, 0.0)
            spread[lanes_of(block), span] = hit.astype(SMALL)
        return carry

    lax.fori_loop(0, width // LANES, build_spread, 0)

    step_width = min(512, width)
    spans = [slice(first, first + step_width) for first in range(0, width, step_width)]

    def match(span):
        for who in range(PLAYERS):
            positive = [
                jnp.maximum(regret[who * ACTIONS + act, :, span], 0.0) for act in range(ACTIONS)
            ]
            total = (positive[0] + positive[1]) + (positive[2] + positive[3])
            inverse = 1.0 / (total + ACTIONS * SMOOTH)
            for act in range(ACTIONS):
                sigma[who * ACTIONS + act, :, span] = (positive[act] + SMOOTH) * inverse

    totals = jnp.zeros((ROWS, 1), jnp.float32)
    for turn_of, distance in enumerate([0] + outward[:-1]):
        if turn_of == chips // 2:
            await_bytes(regret, regret_recv)
            for span in spans:
                match(span)
        arrived = far.at[0, :, pl.ds(0, LANES)] if distance == 0 else far.at[0]
        await_bytes(arrived, far_recv.at[distance])
        source = (chip + chips - distance) % chips
        rows = pl.ds(pl.multiple_of(source * CORES * LANES, CORES * LANES), CORES * LANES)
        panel = far[source]
        for span in spans:
            now = times(panel, onehot[rows, span])
            if turn_of > 0:
                now = now + lifted[:, span]
            if turn_of < chips - 1:
                lifted[:, span] = now
            else:
                now = (now * sigma[:, :, span].reshape(ROWS, step_width)).astype(jnp.bfloat16)
                reach[:, span] = now
                totals = totals + jnp.sum(now.astype(jnp.float32), axis=1, keepdims=True)

    def opponent(rows):
        return jnp.concatenate([rows[ROWS // 2 :], rows[: ROWS // 2]], axis=0)

    await_bytes(meta.at[pl.ds(1, SLOTS - 1)], meta_recv)
    pot_here = meta[:, :, :LANES].reshape(ROWS, LANES) * scale
    code_here = meta[:, :, LANES:].reshape(ROWS, LANES)
    row = lax.broadcasted_iota(jnp.int32, (ROWS, LANES), 0)
    who_here = jnp.where(row >= ROWS // 2, 1.0, 0.0)
    signed = jnp.where(code_here == who_here, -pot_here, pot_here)
    fold = signed * opponent(totals)
    repeats = step_width // LANES
    fold_wide = jnp.concatenate([fold] * repeats, axis=1)
    pot_wide = jnp.concatenate([pot_here] * repeats, axis=1)
    show_wide = jnp.concatenate([code_here] * repeats, axis=1) == 2.0

    for span in spans:
        equity = times(reach[...], strength[:, span])
        value = jnp.where(show_wide, pot_wide * opponent(equity), fold_wide)
        updated[:, :, span] = value.reshape(SLOTS, CHUNK, step_width)
        share = sigma[:, :, span].reshape(ROWS, step_width) * value
        weighted[:, span] = share.astype(jnp.bfloat16)

    def renew(tile, carry):
        span = lanes_of(tile)
        for who in range(PLAYERS):
            those = [who * ACTIONS + act for act in range(ACTIONS)]
            value = [updated[index, :, span] for index in those]
            share = [sigma[index, :, span] * now for index, now in zip(those, value)]
            node = (share[0] + share[1]) + (share[2] + share[3])
            for index, now in zip(those, value):
                updated[index, :, span] = (regret[index, :, span] + now) - node
        return carry

    keep_fresh = pltpu.make_async_copy(updated.at[slot], fresh.at[chunk_of(chunk)], fresh_recv)

    for turn_of, there in enumerate([0, 1, 2, 3, 4, 5, 6, 7]):
        if turn_of == chips // 2:
            lax.fori_loop(0, width // LANES, renew, 0)
            each(SLOTS, lambda step: fresh_copy(step).start())
            keep_fresh.start()
        columns_there = slice(there * CORES * LANES, (there + 1) * CORES * LANES)
        block = times(weighted[...], spread[:, columns_there])
        back_out[there] = block.astype(jnp.bfloat16)
        for mate in reversed(range(CORES)):

            @pl.when(place != there * CORES + mate)
            def send_back(there=there, mate=mate):
                back_copy(there, mate).start()

    back[place] = back_out[chip, :, lanes_of(core)]

    held = [jnp.zeros((ROWS, LANES), jnp.float32) for unused in range(CLUSTERS)]
    await_bytes(back.at[pl.ds(1, ring - 1)], back_recv)
    for source in range(ring):
        block = back[source].astype(jnp.float32)
        theirs = clusters[source]
        for index in range(CLUSTERS):
            held[index] = held[index] + jnp.where(theirs == index, block, 0.0)
    held = [part.reshape(SLOTS, CHUNK, LANES) for part in held]
    for pair in range(CLUSTERS // 2):
        rows = slice(pair * CHUNK, (pair + 1) * CHUNK)
        first, second = held[2 * pair], held[2 * pair + 1]
        last_out[:SLOTS, rows] = jnp.where(low, first, pltpu.roll(second, PIECE, 2))
        last_out[SLOTS:, rows] = jnp.where(low, pltpu.roll(first, PIECE, 2), second)

    def lateness(there):
        return there // SLOTS * PLAYERS + there % PLAYERS + there % SLOTS // PLAYERS

    for there in sorted(range(HALVES * SLOTS), key=lateness):

        @pl.when(there != half * SLOTS + chunk)
        def send_last(there=there):
            last_copy(there).start()

    last[half * SLOTS + chunk] = last_out[half * SLOTS + slot]

    await_bytes(clusters.at[pl.ds(1, ring - 1)], cluster_send)
    await_bytes(far_out.at[pl.ds(1, ring - 1)], far_send)
    await_bytes(back.at[pl.ds(1, ring - 1)], back_send)
    await_bytes(regret.at[pl.ds(1, SLOTS - 1)], regret_send)
    await_bytes(meta.at[pl.ds(1, SLOTS - 1)], meta_send)
    await_bytes(near.at[pl.ds(1, HALVES * SLOTS - 1)], near_send)
    await_bytes(updated.at[pl.ds(1, SLOTS - 1)], fresh_send)
    await_bytes(updated, fresh_recv)

    await_bytes(last.at[pl.ds(1, HALVES * SLOTS - 1)], last_recv)
    total = last[:SLOTS] + last[SLOTS:]
    for pair in range(CLUSTERS // 2):
        rows = slice(pair * CHUNK, (pair + 1) * CHUNK)
        both = total[:, rows].reshape(nodes, 2 * PIECE).T
        shares[:, 2 * pair, :] = both[:PIECE]
        shares[:, 2 * pair + 1, :] = both[PIECE:]
    await_bytes(last.at[pl.ds(1, HALVES * SLOTS - 1)], last_send)


def on_device(ring, turn_reach, regrets, pot, turn_cluster, bucket_map, codes, ranks):
    width = ranks.shape[1]
    depth = ring * LANES
    near = HALVES * SLOTS
    nodes = SLOTS * CHUNK
    chips = ring // CORES
    tile = (CLUSTERS // 2 * CHUNK, 2 * PIECE)
    vmem = pl.BlockSpec(memory_space=pltpu.VMEM)
    hbm = pl.BlockSpec(memory_space=pltpu.HBM)
    dma = pltpu.SemaphoreType.DMA
    fresh, shares = pl.pallas_call(
        kernel,
        out_shape=(
            jax.ShapeDtypeStruct((nodes, width), jnp.float32),
            jax.ShapeDtypeStruct((PIECE, CLUSTERS, nodes), jnp.float32),
        ),
        in_specs=[hbm, hbm, hbm, hbm, pl.BlockSpec(memory_space=pltpu.SMEM), hbm, hbm],
        out_specs=(hbm, vmem),
        scratch_shapes=[
            pltpu.VMEM((depth, width), SMALL),
            pltpu.VMEM((width, depth), SMALL),
            pltpu.VMEM((width, width), SMALL),
            pltpu.VMEM((PIECE, CLUSTERS, nodes), jnp.bfloat16),
            pltpu.VMEM((PIECE, CLUSTERS, nodes), jnp.float32),
            pltpu.VMEM((SLOTS, *tile), jnp.bfloat16),
            pltpu.VMEM((1, nodes), jnp.float32),
            pltpu.VMEM((1, nodes), jnp.int32),
            pltpu.VMEM((1, width), jnp.int32),
            pltpu.VMEM((1, width), jnp.int32),
            pltpu.VMEM((SLOTS, CHUNK, 2 * LANES), jnp.float32),
            pltpu.VMEM((SLOTS, CHUNK, 2 * LANES), jnp.float32),
            pltpu.VMEM((SLOTS, CHUNK, width), jnp.float32),
            pltpu.VMEM((SLOTS, CHUNK, width), jnp.float32),
            pltpu.VMEM((near, *tile), jnp.bfloat16),
            pltpu.VMEM((1, LANES), jnp.int32),
            pltpu.VMEM((ring, 1, LANES), jnp.int32),
            pltpu.VMEM((ring, ROWS, LANES), jnp.bfloat16),
            pltpu.VMEM((chips, ROWS, CORES * LANES), jnp.bfloat16),
            pltpu.VMEM((ROWS, width), jnp.float32),
            pltpu.VMEM((ROWS, width), jnp.bfloat16),
            pltpu.VMEM((SLOTS, CHUNK, width), jnp.float32),
            pltpu.VMEM((ROWS, width), jnp.bfloat16),
            pltpu.VMEM((chips, ROWS, CORES * LANES), jnp.bfloat16),
            pltpu.VMEM((ring, ROWS, LANES), jnp.bfloat16),
            pltpu.VMEM((near, *tile), jnp.float32),
            pltpu.VMEM((near, *tile), jnp.float32),
            dma((5,)),
            dma,
            dma,
            dma,
            dma,
            dma,
            dma,
            dma,
            dma,
            dma,
            dma((chips,)),
            dma,
            dma,
            dma,
            dma,
            dma,
            dma,
        ],
        compiler_params=pltpu.CompilerParams(
            collective_id=0, has_side_effects=True, vmem_limit_bytes=32 * 2**20
        ),
    )(
        *(
            pltpu.with_memory_space_constraint(x, pltpu.HBM)
            for x in (regrets[0, 0], turn_reach[0], pot[None], codes[None])
        ),
        turn_cluster,
        *(pltpu.with_memory_space_constraint(x, pltpu.HBM) for x in (bucket_map, ranks)),
    )
    return fresh[None, None], shares[None]


def solution(mesh):
    return jax.shard_map(
        functools.partial(on_device, mesh.shape["board"] // HALVES),
        mesh=mesh,
        in_specs=(
            P("pair", "board", None, "hist"),
            P("pair", "board", "hist", None),
            P("hist"),
            P("board"),
            P("board", None),
            P("hist"),
            P("board", None),
        ),
        out_specs=(P("pair", "board", "hist", None), P("pair", "board", None, "hist")),
        check_vma=False,
    )
```

```python
import functools

import jax
import jax.numpy as jnp
from jax import lax
from jax.experimental import pallas as pl
from jax.experimental.pallas import tpu as pltpu
from jax.sharding import PartitionSpec as P

ACTIONS = 4
CLUSTERS = 4
PLAYERS = 2
SMOOTH = 0.01
CHUNK = 8
SLOTS = PLAYERS * ACTIONS
ROWS = SLOTS * CHUNK
HALVES = 2
PIECE = 64
CORES = 2
LANES = 128
MESH = pl.DeviceIdType.MESH
SMALL = jnp.float8_e4m3fn


def times(rows, matrix):
    return lax.dot_general(
        rows, matrix, (((1,), (0,)), ((), ())), preferred_element_type=jnp.float32
    )


def kernel(
    regrets,
    turn_reach,
    pot,
    codes,
    cluster,
    mapping,
    ranks,
    fresh,
    shares,
    onehot,
    spread,
    strength,
    turn_raw,
    turn_rows,
    turn,
    pot_row,
    code_row,
    map_row,
    rank_row,
    meta_out,
    meta,
    regret,
    sigma,
    near,
    cluster_out,
    clusters,
    far_out,
    far,
    lifted,
    reach,
    updated,
    weighted,
    back_out,
    back,
    last_out,
    last,
    fetch_sem,
    regret_send,
    regret_recv,
    meta_send,
    meta_recv,
    near_send,
    near_recv,
    cluster_send,
    cluster_recv,
    far_send,
    far_recv,
    fresh_send,
    fresh_recv,
    back_send,
    back_recv,
    last_send,
    last_recv,
):
    width = ranks.shape[1]
    ring = back.shape[0]
    chips = ring // CORES
    board = lax.axis_index("board")
    action = lax.axis_index("hist")
    player = lax.axis_index("pair")
    half = board // ring
    place = board % ring
    chip = place // CORES
    core = place % CORES
    chunk = action * PLAYERS + player
    slot = player * ACTIONS + action
    scale = width ** (-0.5)
    inward = [(i + 1) // 2 if i % 2 else (chips - i // 2) % chips for i in range(chips)]
    outward = inward[::-1]

    def same_board(step):
        other = (chunk + step) % SLOTS
        return other, {"board": board, "hist": other // PLAYERS, "pair": other % PLAYERS}

    def near_peer(step):
        their_half = (half + step // SLOTS) % HALVES
        their_action = (action + step % SLOTS // PLAYERS) % ACTIONS
        their_player = (player + step) % PLAYERS
        their_chunk = their_action * PLAYERS + their_player
        their_slot = their_player * ACTIONS + their_action
        target = {
            "board": their_half * ring + place,
            "hist": their_action,
            "pair": their_player,
        }
        return their_half, their_chunk, their_slot, target

    def hops(step):
        along = step % SLOTS // PLAYERS
        across = 1 if step % PLAYERS else 2 * (step // SLOTS)
        return min(along, ACTIONS - along) + across

    near_steps = sorted(range(1, HALVES * SLOTS), key=hops, reverse=True)
    far_steps = [
        step
        for distance in outward
        for step in range(distance * CORES, (distance + 1) * CORES)
        if step > 0
    ]

    def far_peer(step):
        there = (chip + step // CORES) % chips
        mate = (core + step) % CORES
        other = there * CORES + mate
        target = {"board": half * ring + other, "hist": action, "pair": player}
        return there, mate, other, target

    def lanes_of(index):
        return pl.ds(pl.multiple_of(index * LANES, LANES), LANES)

    def chunk_of(index):
        return pl.ds(pl.multiple_of(index * CHUNK, CHUNK), CHUNK)

    def remote(src, dst, send, recv, target):
        return pltpu.make_async_remote_copy(
            src_ref=src,
            dst_ref=dst,
            send_sem=send,
            recv_sem=recv,
            device_id=target,
            device_id_type=MESH,
        )

    def await_bytes(buffer, semaphore):
        pltpu.make_async_copy(buffer, buffer, semaphore).wait()

    def regret_copy(step):
        other, target = same_board(step)
        return remote(
            regrets.at[chunk_of(other)], regret.at[slot], regret_send, regret_recv, target
        )

    def meta_copy(step):
        other, target = same_board(step)
        return remote(meta_out.at[other], meta.at[slot], meta_send, meta_recv, target)

    def near_copy(step):
        their_half, their_chunk, their_slot, target = near_peer(step)
        return remote(
            turn.at[their_chunk],
            near.at[half * SLOTS + slot],
            near_send,
            near_recv,
            target,
        )

    def cluster_copy(step):
        there, mate, other, target = far_peer(step)
        return remote(cluster_out, clusters.at[place], cluster_send, cluster_recv, target)

    def far_copy(step):
        there, mate, other, target = far_peer(step)
        return remote(
            far_out.at[other],
            far.at[chip, :, lanes_of(core)],
            far_send,
            far_recv.at[step // CORES],
            target,
        )

    def fresh_copy(step):
        other, target = same_board(step)
        their_slot = (other % PLAYERS) * ACTIONS + other // PLAYERS
        return remote(
            updated.at[their_slot],
            fresh.at[chunk_of(chunk)],
            fresh_send,
            fresh_recv,
            target,
        )

    def back_copy(there, mate):
        target = {"board": half * ring + there * CORES + mate, "hist": action, "pair": player}
        return remote(
            back_out.at[there, :, lanes_of(mate)],
            back.at[place],
            back_send,
            back_recv,
            target,
        )

    def last_copy(there):
        their_half, rest = there // SLOTS, there % SLOTS
        their_action, their_player = rest // PLAYERS, rest % PLAYERS
        their_slot = their_player * ACTIONS + their_action
        target = {
            "board": their_half * ring + place,
            "hist": their_action,
            "pair": their_player,
        }
        return remote(
            last_out.at[their_half * SLOTS + their_slot],
            last.at[half * SLOTS + chunk],
            last_send,
            last_recv,
            target,
        )

    def each(count, action_of):
        def body(step, carry):
            action_of(step)
            return carry

        lax.fori_loop(1, count, body, 0)

    sources = [
        (turn_reach, turn_raw, fetch_sem.at[0]),
        (pot, pot_row, fetch_sem.at[1]),
        (codes, code_row, fetch_sem.at[2]),
        (ranks, rank_row, fetch_sem.at[3]),
        (mapping, map_row, fetch_sem.at[4]),
        (regrets.at[chunk_of(chunk)], regret.at[slot], regret_recv),
    ]
    fetches = [pltpu.make_async_copy(*source) for source in sources]
    fetches[0].start()

    barrier = pltpu.get_barrier_semaphore()

    def greet_near(step):
        target = near_peer(step)[-1]
        pl.semaphore_signal(barrier, inc=1, device_id=target, device_id_type=MESH)

    def greet_far(step):
        target = far_peer(step)[-1]
        pl.semaphore_signal(barrier, inc=1, device_id=target, device_id_type=MESH)

    for step in near_steps:
        greet_near(step)
    for step in far_steps:
        greet_far(step)
    for fetch in fetches[1:]:
        fetch.start()

    own_cluster = jnp.full((1, LANES), cluster[0], jnp.int32)
    cluster_out[...] = own_cluster
    clusters[place] = own_cluster
    for fetch in fetches[:3]:
        fetch.wait()
    nodes = SLOTS * CHUNK
    turn_rows[...] = turn_raw[...].astype(jnp.float32)
    columns = []
    for pair in range(CLUSTERS // 2):
        both = jnp.concatenate([turn_rows[:, 2 * pair, :], turn_rows[:, 2 * pair + 1, :]], axis=0)
        columns.append(both.T.reshape(SLOTS, CHUNK, 2 * PIECE))
    turn[...] = jnp.concatenate(columns, axis=1).astype(jnp.bfloat16)
    line = lax.broadcasted_iota(jnp.int32, (nodes, nodes), 0)
    column = lax.broadcasted_iota(jnp.int32, (nodes, nodes), 1)
    diagonal = line == column
    pot_rows = jnp.sum(jnp.where(diagonal, pot_row[...], 0.0), axis=1, keepdims=True)
    code_rows = jnp.sum(
        jnp.where(diagonal, code_row[...].astype(jnp.float32), 0.0), axis=1, keepdims=True
    )
    meta_out[:, :, :LANES] = jnp.broadcast_to(pot_rows, (nodes, LANES)).reshape(
        SLOTS, CHUNK, LANES
    )
    meta_out[:, :, LANES:] = jnp.broadcast_to(code_rows, (nodes, LANES)).reshape(
        SLOTS, CHUNK, LANES
    )
    near[half * SLOTS + slot] = turn[chunk]
    meta[slot] = meta_out[chunk]
    pl.semaphore_wait(barrier, HALVES * SLOTS - 1 + ring - 1)

    for step in near_steps:
        near_copy(step).start()
    for step in far_steps:
        cluster_copy(step).start()
    each(SLOTS, lambda step: meta_copy(step).start())

    for fetch in fetches[3:5]:
        fetch.wait()
    rank_wide = rank_row[...].astype(jnp.float32)

    def build_strength(block, carry):
        mine = rank_row[:, lanes_of(block)].astype(jnp.float32)
        rank_column = jnp.broadcast_to(mine, (LANES, LANES)).T
        for tile in range(width // LANES):
            span = slice(tile * LANES, (tile + 1) * LANES)
            sign = jnp.minimum(jnp.maximum(rank_wide[:, span] - rank_column, -1.0), 1.0)
            strength[lanes_of(block), span] = sign.astype(SMALL)
        return carry

    lax.fori_loop(0, width // LANES, build_strength, 0)

    each(SLOTS, lambda step: regret_copy(step).start())

    await_bytes(near.at[pl.ds(1, HALVES * SLOTS - 1)], near_recv)
    await_bytes(clusters.at[pl.ds(1, ring - 1)], cluster_recv)
    low = lax.broadcasted_iota(jnp.int32, (SLOTS, CHUNK, LANES), 2) < PIECE
    parts = []
    lower = near[:SLOTS].astype(jnp.float32)
    upper = near[SLOTS:].astype(jnp.float32)
    for pair in range(CLUSTERS // 2):
        rows = slice(pair * CHUNK, (pair + 1) * CHUNK)
        first, second = lower[:, rows], upper[:, rows]
        parts.append(jnp.where(low, first, pltpu.roll(second, PIECE, 2)))
        parts.append(jnp.where(low, pltpu.roll(first, PIECE, 2), second))
    panels = [part.reshape(ROWS, LANES) for part in parts]

    def choose(other):
        wanted = clusters[other]
        result = panels[0]
        for index in range(1, CLUSTERS):
            result = jnp.where(wanted == index, panels[index], result)
        return result.astype(jnp.bfloat16)

    for step in far_steps:
        other = far_peer(step)[2]
        far_out[other] = choose(other)
        far_copy(step).start()
    far[chip, :, lanes_of(core)] = choose(place)

    bucket = map_row[...]
    shard, within = bucket // PIECE, bucket % PIECE
    map_row[...] = (shard % ring) * LANES + (shard // ring) * PIECE + within
    map_wide = map_row[...]
    tiles = ring * LANES // LANES

    def build_onehot(block, carry):
        index = lax.broadcasted_iota(jnp.int32, (LANES, LANES), 0) + block * LANES
        for tile in range(width // LANES):
            span = slice(tile * LANES, (tile + 1) * LANES)
            hit = jnp.where(map_wide[:, span] == index, 1.0, 0.0)
            onehot[lanes_of(block), span] = hit.astype(SMALL)
        return carry

    lax.fori_loop(0, tiles, build_onehot, 0)

    def build_spread(block, carry):
        mine = map_row[:, lanes_of(block)].astype(jnp.float32)
        map_column = jnp.broadcast_to(mine, (LANES, LANES)).T.astype(jnp.int32)
        index = lax.broadcasted_iota(jnp.int32, (LANES, LANES), 1)
        for tile in range(tiles):
            span = slice(tile * LANES, (tile + 1) * LANES)
            hit = jnp.where(map_column == index + tile * LANES, 1.0, 0.0)
            spread[lanes_of(block), span] = hit.astype(SMALL)
        return carry

    lax.fori_loop(0, width // LANES, build_spread, 0)

    step_width = min(512, width)
    spans = [slice(first, first + step_width) for first in range(0, width, step_width)]

    def match(span):
        for who in range(PLAYERS):
            positive = [
                jnp.maximum(regret[who * ACTIONS + act, :, span], 0.0) for act in range(ACTIONS)
            ]
            total = (positive[0] + positive[1]) + (positive[2] + positive[3])
            inverse = 1.0 / (total + ACTIONS * SMOOTH)
            for act in range(ACTIONS):
                sigma[who * ACTIONS + act, :, span] = (positive[act] + SMOOTH) * inverse

    totals = jnp.zeros((ROWS, 1), jnp.float32)
    for turn_of, distance in enumerate([0] + outward[:-1]):
        if turn_of == chips // 2:
            await_bytes(regret, regret_recv)
            for span in spans:
                match(span)
        arrived = far.at[0, :, pl.ds(0, LANES)] if distance == 0 else far.at[0]
        await_bytes(arrived, far_recv.at[distance])
        source = (chip + chips - distance) % chips
        rows = pl.ds(pl.multiple_of(source * CORES * LANES, CORES * LANES), CORES * LANES)
        panel = far[source]
        for span in spans:
            now = times(panel, onehot[rows, span])
            if turn_of > 0:
                now = now + lifted[:, span]
            if turn_of < chips - 1:
                lifted[:, span] = now
            else:
                now = (now * sigma[:, :, span].reshape(ROWS, step_width)).astype(jnp.bfloat16)
                reach[:, span] = now
                totals = totals + jnp.sum(now.astype(jnp.float32), axis=1, keepdims=True)

    def opponent(rows):
        return jnp.concatenate([rows[ROWS // 2 :], rows[: ROWS // 2]], axis=0)

    await_bytes(meta.at[pl.ds(1, SLOTS - 1)], meta_recv)
    pot_here = meta[:, :, :LANES].reshape(ROWS, LANES) * scale
    code_here = meta[:, :, LANES:].reshape(ROWS, LANES)
    row = lax.broadcasted_iota(jnp.int32, (ROWS, LANES), 0)
    who_here = jnp.where(row >= ROWS // 2, 1.0, 0.0)
    signed = jnp.where(code_here == who_here, -pot_here, pot_here)
    fold = signed * opponent(totals)
    repeats = step_width // LANES
    fold_wide = jnp.concatenate([fold] * repeats, axis=1)
    pot_wide = jnp.concatenate([pot_here] * repeats, axis=1)
    show_wide = jnp.concatenate([code_here] * repeats, axis=1) == 2.0

    for span in spans:
        equity = times(reach[...], strength[:, span])
        value = jnp.where(show_wide, pot_wide * opponent(equity), fold_wide)
        updated[:, :, span] = value.reshape(SLOTS, CHUNK, step_width)
        share = sigma[:, :, span].reshape(ROWS, step_width) * value
        weighted[:, span] = share.astype(jnp.bfloat16)

    def renew(tile, carry):
        span = lanes_of(tile)
        for who in range(PLAYERS):
            those = [who * ACTIONS + act for act in range(ACTIONS)]
            value = [updated[index, :, span] for index in those]
            share = [sigma[index, :, span] * now for index, now in zip(those, value)]
            node = (share[0] + share[1]) + (share[2] + share[3])
            for index, now in zip(those, value):
                updated[index, :, span] = (regret[index, :, span] + now) - node
        return carry

    keep_fresh = pltpu.make_async_copy(updated.at[slot], fresh.at[chunk_of(chunk)], fresh_recv)

    for turn_of, there in enumerate([0, 1, 2, 3, 4, 5, 6, 7]):
        if turn_of == chips // 2:
            lax.fori_loop(0, width // LANES, renew, 0)
            each(SLOTS, lambda step: fresh_copy(step).start())
            keep_fresh.start()
        columns_there = slice(there * CORES * LANES, (there + 1) * CORES * LANES)
        block = times(weighted[...], spread[:, columns_there])
        back_out[there] = block.astype(jnp.bfloat16)
        if turn_of % 2:
            for one, mate in ((there - 1, 1), (there, 1), (there - 1, 0), (there, 0)):

                @pl.when(place != one * CORES + mate)
                def send_back(one=one, mate=mate):
                    back_copy(one, mate).start()

    back[place] = back_out[chip, :, lanes_of(core)]

    held = [jnp.zeros((ROWS, LANES), jnp.float32) for unused in range(CLUSTERS)]
    await_bytes(back.at[pl.ds(1, ring - 1)], back_recv)
    for source in range(ring):
        block = back[source].astype(jnp.float32)
        theirs = clusters[source]
        for index in range(CLUSTERS):
            held[index] = held[index] + jnp.where(theirs == index, block, 0.0)
    held = [part.reshape(SLOTS, CHUNK, LANES) for part in held]
    for pair in range(CLUSTERS // 2):
        rows = slice(pair * CHUNK, (pair + 1) * CHUNK)
        first, second = held[2 * pair], held[2 * pair + 1]
        last_out[:SLOTS, rows] = jnp.where(low, first, pltpu.roll(second, PIECE, 2))
        last_out[SLOTS:, rows] = jnp.where(low, pltpu.roll(first, PIECE, 2), second)

    def lateness(there):
        return there // SLOTS * PLAYERS + there % PLAYERS + there % SLOTS // PLAYERS

    for there in sorted(range(HALVES * SLOTS), key=lateness):

        @pl.when(there != half * SLOTS + chunk)
        def send_last(there=there):
            last_copy(there).start()

    last[half * SLOTS + chunk] = last_out[half * SLOTS + slot]

    await_bytes(clusters.at[pl.ds(1, ring - 1)], cluster_send)
    await_bytes(far_out.at[pl.ds(1, ring - 1)], far_send)
    await_bytes(back.at[pl.ds(1, ring - 1)], back_send)
    await_bytes(regret.at[pl.ds(1, SLOTS - 1)], regret_send)
    await_bytes(meta.at[pl.ds(1, SLOTS - 1)], meta_send)
    await_bytes(near.at[pl.ds(1, HALVES * SLOTS - 1)], near_send)
    await_bytes(updated.at[pl.ds(1, SLOTS - 1)], fresh_send)
    await_bytes(updated, fresh_recv)

    await_bytes(last.at[pl.ds(1, HALVES * SLOTS - 1)], last_recv)
    total = last[:SLOTS] + last[SLOTS:]
    for pair in range(CLUSTERS // 2):
        rows = slice(pair * CHUNK, (pair + 1) * CHUNK)
        both = total[:, rows].reshape(nodes, 2 * PIECE).T
        shares[:, 2 * pair, :] = both[:PIECE]
        shares[:, 2 * pair + 1, :] = both[PIECE:]
    await_bytes(last.at[pl.ds(1, HALVES * SLOTS - 1)], last_send)


def on_device(ring, turn_reach, regrets, pot, turn_cluster, bucket_map, codes, ranks):
    width = ranks.shape[1]
    depth = ring * LANES
    near = HALVES * SLOTS
    nodes = SLOTS * CHUNK
    chips = ring // CORES
    tile = (CLUSTERS // 2 * CHUNK, 2 * PIECE)
    vmem = pl.BlockSpec(memory_space=pltpu.VMEM)
    hbm = pl.BlockSpec(memory_space=pltpu.HBM)
    dma = pltpu.SemaphoreType.DMA
    fresh, shares = pl.pallas_call(
        kernel,
        out_shape=(
            jax.ShapeDtypeStruct((nodes, width), jnp.float32),
            jax.ShapeDtypeStruct((PIECE, CLUSTERS, nodes), jnp.float32),
        ),
        in_specs=[hbm, hbm, hbm, hbm, pl.BlockSpec(memory_space=pltpu.SMEM), hbm, hbm],
        out_specs=(hbm, vmem),
        scratch_shapes=[
            pltpu.VMEM((depth, width), SMALL),
            pltpu.VMEM((width, depth), SMALL),
            pltpu.VMEM((width, width), SMALL),
            pltpu.VMEM((PIECE, CLUSTERS, nodes), jnp.bfloat16),
            pltpu.VMEM((PIECE, CLUSTERS, nodes), jnp.float32),
            pltpu.VMEM((SLOTS, *tile), jnp.bfloat16),
            pltpu.VMEM((1, nodes), jnp.float32),
            pltpu.VMEM((1, nodes), jnp.int32),
            pltpu.VMEM((1, width), jnp.int32),
            pltpu.VMEM((1, width), jnp.int32),
            pltpu.VMEM((SLOTS, CHUNK, 2 * LANES), jnp.float32),
            pltpu.VMEM((SLOTS, CHUNK, 2 * LANES), jnp.float32),
            pltpu.VMEM((SLOTS, CHUNK, width), jnp.float32),
            pltpu.VMEM((SLOTS, CHUNK, width), jnp.float32),
            pltpu.VMEM((near, *tile), jnp.bfloat16),
            pltpu.VMEM((1, LANES), jnp.int32),
            pltpu.VMEM((ring, 1, LANES), jnp.int32),
            pltpu.VMEM((ring, ROWS, LANES), jnp.bfloat16),
            pltpu.VMEM((chips, ROWS, CORES * LANES), jnp.bfloat16),
            pltpu.VMEM((ROWS, width), jnp.float32),
            pltpu.VMEM((ROWS, width), jnp.bfloat16),
            pltpu.VMEM((SLOTS, CHUNK, width), jnp.float32),
            pltpu.VMEM((ROWS, width), jnp.bfloat16),
            pltpu.VMEM((chips, ROWS, CORES * LANES), jnp.bfloat16),
            pltpu.VMEM((ring, ROWS, LANES), jnp.bfloat16),
            pltpu.VMEM((near, *tile), jnp.float32),
            pltpu.VMEM((near, *tile), jnp.float32),
            dma((5,)),
            dma,
            dma,
            dma,
            dma,
            dma,
            dma,
            dma,
            dma,
            dma,
            dma((chips,)),
            dma,
            dma,
            dma,
            dma,
            dma,
            dma,
        ],
        compiler_params=pltpu.CompilerParams(
            collective_id=0, has_side_effects=True, vmem_limit_bytes=32 * 2**20
        ),
    )(
        *(
            pltpu.with_memory_space_constraint(x, pltpu.HBM)
            for x in (regrets[0, 0], turn_reach[0], pot[None], codes[None])
        ),
        turn_cluster,
        *(pltpu.with_memory_space_constraint(x, pltpu.HBM) for x in (bucket_map, ranks)),
    )
    return fresh[None, None], shares[None]


def solution(mesh):
    return jax.shard_map(
        functools.partial(on_device, mesh.shape["board"] // HALVES),
        mesh=mesh,
        in_specs=(
            P("pair", "board", None, "hist"),
            P("pair", "board", "hist", None),
            P("hist"),
            P("board"),
            P("board", None),
            P("hist"),
            P("board", None),
        ),
        out_specs=(P("pair", "board", "hist", None), P("pair", "board", None, "hist")),
        check_vma=False,
    )
```

```python
import functools

import jax
import jax.numpy as jnp
from jax import lax
from jax.experimental import pallas as pl
from jax.experimental.pallas import tpu as pltpu
from jax.sharding import PartitionSpec as P

ACTIONS = 4
CLUSTERS = 4
PLAYERS = 2
SMOOTH = 0.01
CHUNK = 8
SLOTS = PLAYERS * ACTIONS
ROWS = SLOTS * CHUNK
HALVES = 2
PIECE = 64
CORES = 2
LANES = 128
MESH = pl.DeviceIdType.MESH
SMALL = jnp.float8_e4m3fn


def times(rows, matrix):
    return lax.dot_general(
        rows, matrix, (((1,), (0,)), ((), ())), preferred_element_type=jnp.float32
    )


def kernel(
    regrets,
    turn_reach,
    pot,
    codes,
    cluster,
    mapping,
    ranks,
    fresh,
    shares,
    onehot,
    spread,
    strength,
    turn_raw,
    turn_rows,
    turn,
    pot_row,
    code_row,
    map_row,
    rank_row,
    meta_out,
    meta,
    regret,
    sigma,
    near,
    cluster_out,
    clusters,
    far_out,
    far,
    lifted,
    reach,
    updated,
    weighted,
    back_out,
    back,
    last_out,
    last,
    fetch_sem,
    regret_send,
    regret_recv,
    meta_send,
    meta_recv,
    near_send,
    near_recv,
    cluster_send,
    cluster_recv,
    far_send,
    far_recv,
    fresh_send,
    fresh_recv,
    back_send,
    back_recv,
    last_send,
    last_recv,
):
    width = ranks.shape[1]
    ring = back.shape[0]
    chips = ring // CORES
    board = lax.axis_index("board")
    action = lax.axis_index("hist")
    player = lax.axis_index("pair")
    half = board // ring
    place = board % ring
    chip = place // CORES
    core = place % CORES
    chunk = action * PLAYERS + player
    slot = player * ACTIONS + action
    scale = width ** (-0.5)
    inward = [(i + 1) // 2 if i % 2 else (chips - i // 2) % chips for i in range(chips)]
    outward = inward[::-1]

    def same_board(step):
        other = (chunk + step) % SLOTS
        return other, {"board": board, "hist": other // PLAYERS, "pair": other % PLAYERS}

    def near_peer(step):
        their_half = (half + step // SLOTS) % HALVES
        their_action = (action + step % SLOTS // PLAYERS) % ACTIONS
        their_player = (player + step) % PLAYERS
        their_chunk = their_action * PLAYERS + their_player
        their_slot = their_player * ACTIONS + their_action
        target = {
            "board": their_half * ring + place,
            "hist": their_action,
            "pair": their_player,
        }
        return their_half, their_chunk, their_slot, target

    def hops(step):
        along = step % SLOTS // PLAYERS
        across = 1 if step % PLAYERS else 2 * (step // SLOTS)
        return min(along, ACTIONS - along) + across

    near_steps = sorted(range(1, HALVES * SLOTS), key=hops, reverse=True)
    far_steps = [
        step
        for distance in outward
        for step in range(distance * CORES, (distance + 1) * CORES)
        if step > 0
    ]

    def far_peer(step):
        there = (chip + step // CORES) % chips
        mate = (core + step) % CORES
        other = there * CORES + mate
        target = {"board": half * ring + other, "hist": action, "pair": player}
        return there, mate, other, target

    def lanes_of(index):
        return pl.ds(pl.multiple_of(index * LANES, LANES), LANES)

    def chunk_of(index):
        return pl.ds(pl.multiple_of(index * CHUNK, CHUNK), CHUNK)

    def remote(src, dst, send, recv, target):
        return pltpu.make_async_remote_copy(
            src_ref=src,
            dst_ref=dst,
            send_sem=send,
            recv_sem=recv,
            device_id=target,
            device_id_type=MESH,
        )

    def await_bytes(buffer, semaphore):
        pltpu.make_async_copy(buffer, buffer, semaphore).wait()

    def regret_copy(step):
        other, target = same_board(step)
        return remote(
            regrets.at[chunk_of(other)], regret.at[slot], regret_send, regret_recv, target
        )

    def meta_copy(step):
        other, target = same_board(step)
        return remote(meta_out.at[other], meta.at[slot], meta_send, meta_recv, target)

    def near_copy(step):
        their_half, their_chunk, their_slot, target = near_peer(step)
        return remote(
            turn.at[their_chunk],
            near.at[half * SLOTS + slot],
            near_send,
            near_recv,
            target,
        )

    def cluster_copy(step):
        there, mate, other, target = far_peer(step)
        return remote(cluster_out, clusters.at[place], cluster_send, cluster_recv, target)

    def far_copy(step):
        there, mate, other, target = far_peer(step)
        return remote(
            far_out.at[other],
            far.at[chip, :, lanes_of(core)],
            far_send,
            far_recv.at[step // CORES],
            target,
        )

    def fresh_copy(step):
        other, target = same_board(step)
        their_slot = (other % PLAYERS) * ACTIONS + other // PLAYERS
        return remote(
            updated.at[their_slot],
            fresh.at[chunk_of(chunk)],
            fresh_send,
            fresh_recv,
            target,
        )

    def back_copy(there, mate):
        target = {"board": half * ring + there * CORES + mate, "hist": action, "pair": player}
        return remote(
            back_out.at[there, :, lanes_of(mate)],
            back.at[place],
            back_send,
            back_recv,
            target,
        )

    def last_copy(there):
        their_half, rest = there // SLOTS, there % SLOTS
        their_action, their_player = rest // PLAYERS, rest % PLAYERS
        their_slot = their_player * ACTIONS + their_action
        target = {
            "board": their_half * ring + place,
            "hist": their_action,
            "pair": their_player,
        }
        return remote(
            last_out.at[their_half * SLOTS + their_slot],
            last.at[half * SLOTS + chunk],
            last_send,
            last_recv,
            target,
        )

    def each(count, action_of):
        def body(step, carry):
            action_of(step)
            return carry

        lax.fori_loop(1, count, body, 0)

    sources = [
        (turn_reach, turn_raw, fetch_sem.at[0]),
        (pot, pot_row, fetch_sem.at[1]),
        (codes, code_row, fetch_sem.at[2]),
        (ranks, rank_row, fetch_sem.at[3]),
        (mapping, map_row, fetch_sem.at[4]),
        (regrets.at[chunk_of(chunk)], regret.at[slot], regret_recv),
    ]
    fetches = [pltpu.make_async_copy(*source) for source in sources]
    fetches[0].start()

    barrier = pltpu.get_barrier_semaphore()

    def greet_near(step):
        target = near_peer(step)[-1]
        pl.semaphore_signal(barrier, inc=1, device_id=target, device_id_type=MESH)

    def greet_far(step):
        target = far_peer(step)[-1]
        pl.semaphore_signal(barrier, inc=1, device_id=target, device_id_type=MESH)

    around = [(min(step // CORES, chips - step // CORES), False, step) for step in far_steps]
    across = [(hops(step), True, step) for step in near_steps]
    merged = sorted(across + around, key=lambda item: -item[0])

    for distance, in_plane, step in merged:
        if in_plane:
            greet_near(step)
        else:
            greet_far(step)
    for fetch in fetches[1:]:
        fetch.start()

    own_cluster = jnp.full((1, LANES), cluster[0], jnp.int32)
    cluster_out[...] = own_cluster
    clusters[place] = own_cluster
    for fetch in fetches[:3]:
        fetch.wait()
    nodes = SLOTS * CHUNK
    turn_rows[...] = turn_raw[...].astype(jnp.float32)
    columns = []
    for pair in range(CLUSTERS // 2):
        both = jnp.concatenate([turn_rows[:, 2 * pair, :], turn_rows[:, 2 * pair + 1, :]], axis=0)
        columns.append(both.T.reshape(SLOTS, CHUNK, 2 * PIECE))
    turn[...] = jnp.concatenate(columns, axis=1).astype(jnp.bfloat16)
    line = lax.broadcasted_iota(jnp.int32, (nodes, nodes), 0)
    column = lax.broadcasted_iota(jnp.int32, (nodes, nodes), 1)
    diagonal = line == column
    pot_rows = jnp.sum(jnp.where(diagonal, pot_row[...], 0.0), axis=1, keepdims=True)
    code_rows = jnp.sum(
        jnp.where(diagonal, code_row[...].astype(jnp.float32), 0.0), axis=1, keepdims=True
    )
    meta_out[:, :, :LANES] = jnp.broadcast_to(pot_rows, (nodes, LANES)).reshape(
        SLOTS, CHUNK, LANES
    )
    meta_out[:, :, LANES:] = jnp.broadcast_to(code_rows, (nodes, LANES)).reshape(
        SLOTS, CHUNK, LANES
    )
    near[half * SLOTS + slot] = turn[chunk]
    meta[slot] = meta_out[chunk]
    pl.semaphore_wait(barrier, HALVES * SLOTS - 1 + ring - 1)

    for distance, in_plane, step in merged:
        if in_plane:
            near_copy(step).start()
        else:
            cluster_copy(step).start()
    each(SLOTS, lambda step: meta_copy(step).start())

    for fetch in fetches[3:5]:
        fetch.wait()
    rank_wide = rank_row[...].astype(jnp.float32)

    def build_strength(block, carry):
        mine = rank_row[:, lanes_of(block)].astype(jnp.float32)
        rank_column = jnp.broadcast_to(mine, (LANES, LANES)).T
        for tile in range(width // LANES):
            span = slice(tile * LANES, (tile + 1) * LANES)
            sign = jnp.minimum(jnp.maximum(rank_wide[:, span] - rank_column, -1.0), 1.0)
            strength[lanes_of(block), span] = sign.astype(SMALL)
        return carry

    lax.fori_loop(0, width // LANES, build_strength, 0)

    each(SLOTS, lambda step: regret_copy(step).start())

    await_bytes(near.at[pl.ds(1, HALVES * SLOTS - 1)], near_recv)
    await_bytes(clusters.at[pl.ds(1, ring - 1)], cluster_recv)
    low = lax.broadcasted_iota(jnp.int32, (SLOTS, CHUNK, LANES), 2) < PIECE
    parts = []
    lower = near[:SLOTS].astype(jnp.float32)
    upper = near[SLOTS:].astype(jnp.float32)
    for pair in range(CLUSTERS // 2):
        rows = slice(pair * CHUNK, (pair + 1) * CHUNK)
        first, second = lower[:, rows], upper[:, rows]
        parts.append(jnp.where(low, first, pltpu.roll(second, PIECE, 2)))
        parts.append(jnp.where(low, pltpu.roll(first, PIECE, 2), second))
    panels = [part.reshape(ROWS, LANES) for part in parts]

    def choose(other):
        wanted = clusters[other]
        result = panels[0]
        for index in range(1, CLUSTERS):
            result = jnp.where(wanted == index, panels[index], result)
        return result.astype(jnp.bfloat16)

    for step in far_steps:
        other = far_peer(step)[2]
        far_out[other] = choose(other)
        far_copy(step).start()
    far[chip, :, lanes_of(core)] = choose(place)

    bucket = map_row[...]
    shard, within = bucket // PIECE, bucket % PIECE
    map_row[...] = (shard % ring) * LANES + (shard // ring) * PIECE + within
    map_wide = map_row[...]
    tiles = ring * LANES // LANES

    def build_onehot(block, carry):
        index = lax.broadcasted_iota(jnp.int32, (LANES, LANES), 0) + block * LANES
        for tile in range(width // LANES):
            span = slice(tile * LANES, (tile + 1) * LANES)
            hit = jnp.where(map_wide[:, span] == index, 1.0, 0.0)
            onehot[lanes_of(block), span] = hit.astype(SMALL)
        return carry

    lax.fori_loop(0, tiles, build_onehot, 0)

    def build_spread(block, carry):
        mine = map_row[:, lanes_of(block)].astype(jnp.float32)
        map_column = jnp.broadcast_to(mine, (LANES, LANES)).T.astype(jnp.int32)
        index = lax.broadcasted_iota(jnp.int32, (LANES, LANES), 1)
        for tile in range(tiles):
            span = slice(tile * LANES, (tile + 1) * LANES)
            hit = jnp.where(map_column == index + tile * LANES, 1.0, 0.0)
            spread[lanes_of(block), span] = hit.astype(SMALL)
        return carry

    lax.fori_loop(0, width // LANES, build_spread, 0)

    step_width = min(512, width)
    spans = [slice(first, first + step_width) for first in range(0, width, step_width)]

    def match(span):
        for who in range(PLAYERS):
            positive = [
                jnp.maximum(regret[who * ACTIONS + act, :, span], 0.0) for act in range(ACTIONS)
            ]
            total = (positive[0] + positive[1]) + (positive[2] + positive[3])
            inverse = 1.0 / (total + ACTIONS * SMOOTH)
            for act in range(ACTIONS):
                sigma[who * ACTIONS + act, :, span] = (positive[act] + SMOOTH) * inverse

    totals = jnp.zeros((ROWS, 1), jnp.float32)
    for turn_of, distance in enumerate([0] + outward[:-1]):
        if turn_of == chips // 2:
            await_bytes(regret, regret_recv)
            for span in spans:
                match(span)
        arrived = far.at[0, :, pl.ds(0, LANES)] if distance == 0 else far.at[0]
        await_bytes(arrived, far_recv.at[distance])
        source = (chip + chips - distance) % chips
        rows = pl.ds(pl.multiple_of(source * CORES * LANES, CORES * LANES), CORES * LANES)
        panel = far[source]
        for span in spans:
            now = times(panel, onehot[rows, span])
            if turn_of > 0:
                now = now + lifted[:, span]
            if turn_of < chips - 1:
                lifted[:, span] = now
            else:
                now = (now * sigma[:, :, span].reshape(ROWS, step_width)).astype(jnp.bfloat16)
                reach[:, span] = now
                totals = totals + jnp.sum(now.astype(jnp.float32), axis=1, keepdims=True)

    def opponent(rows):
        return jnp.concatenate([rows[ROWS // 2 :], rows[: ROWS // 2]], axis=0)

    await_bytes(meta.at[pl.ds(1, SLOTS - 1)], meta_recv)
    pot_here = meta[:, :, :LANES].reshape(ROWS, LANES) * scale
    code_here = meta[:, :, LANES:].reshape(ROWS, LANES)
    row = lax.broadcasted_iota(jnp.int32, (ROWS, LANES), 0)
    who_here = jnp.where(row >= ROWS // 2, 1.0, 0.0)
    signed = jnp.where(code_here == who_here, -pot_here, pot_here)
    fold = signed * opponent(totals)
    repeats = step_width // LANES
    fold_wide = jnp.concatenate([fold] * repeats, axis=1)
    pot_wide = jnp.concatenate([pot_here] * repeats, axis=1)
    show_wide = jnp.concatenate([code_here] * repeats, axis=1) == 2.0

    for span in spans:
        equity = times(reach[...], strength[:, span])
        value = jnp.where(show_wide, pot_wide * opponent(equity), fold_wide)
        updated[:, :, span] = value.reshape(SLOTS, CHUNK, step_width)
        share = sigma[:, :, span].reshape(ROWS, step_width) * value
        weighted[:, span] = share.astype(jnp.bfloat16)

    def renew(tile, carry):
        span = lanes_of(tile)
        for who in range(PLAYERS):
            those = [who * ACTIONS + act for act in range(ACTIONS)]
            value = [updated[index, :, span] for index in those]
            share = [sigma[index, :, span] * now for index, now in zip(those, value)]
            node = (share[0] + share[1]) + (share[2] + share[3])
            for index, now in zip(those, value):
                updated[index, :, span] = (regret[index, :, span] + now) - node
        return carry

    keep_fresh = pltpu.make_async_copy(updated.at[slot], fresh.at[chunk_of(chunk)], fresh_recv)

    for turn_of, there in enumerate([0, 1, 2, 3, 4, 5, 6, 7]):
        if turn_of == chips // 2:
            lax.fori_loop(0, width // LANES, renew, 0)
            each(SLOTS, lambda step: fresh_copy(step).start())
            keep_fresh.start()
        columns_there = slice(there * CORES * LANES, (there + 1) * CORES * LANES)
        block = times(weighted[...], spread[:, columns_there])
        back_out[there] = block.astype(jnp.bfloat16)
        if turn_of % 2:
            for one, mate in ((there - 1, 1), (there, 1), (there - 1, 0), (there, 0)):

                @pl.when(place != one * CORES + mate)
                def send_back(one=one, mate=mate):
                    back_copy(one, mate).start()

    back[place] = back_out[chip, :, lanes_of(core)]

    held = [jnp.zeros((ROWS, LANES), jnp.float32) for unused in range(CLUSTERS)]
    await_bytes(back.at[pl.ds(1, ring - 1)], back_recv)
    for source in range(ring):
        block = back[source].astype(jnp.float32)
        theirs = clusters[source]
        for index in range(CLUSTERS):
            held[index] = held[index] + jnp.where(theirs == index, block, 0.0)
    held = [part.reshape(SLOTS, CHUNK, LANES) for part in held]
    def lateness(there):
        return there // SLOTS * PLAYERS + there % PLAYERS + there % SLOTS // PLAYERS

    for their_half in range(HALVES):
        for pair in range(CLUSTERS // 2):
            rows = slice(pair * CHUNK, (pair + 1) * CHUNK)
            first, second = held[2 * pair], held[2 * pair + 1]
            if their_half == 0:
                piece = jnp.where(low, first, pltpu.roll(second, PIECE, 2))
            else:
                piece = jnp.where(low, pltpu.roll(first, PIECE, 2), second)
            last_out[their_half * SLOTS : (their_half + 1) * SLOTS, rows] = piece
        theirs = range(their_half * SLOTS, (their_half + 1) * SLOTS)
        for there in sorted(theirs, key=lateness):

            @pl.when(there != half * SLOTS + chunk)
            def send_last(there=there):
                last_copy(there).start()

    last[half * SLOTS + chunk] = last_out[half * SLOTS + slot]

    await_bytes(clusters.at[pl.ds(1, ring - 1)], cluster_send)
    await_bytes(far_out.at[pl.ds(1, ring - 1)], far_send)
    await_bytes(back.at[pl.ds(1, ring - 1)], back_send)
    await_bytes(regret.at[pl.ds(1, SLOTS - 1)], regret_send)
    await_bytes(meta.at[pl.ds(1, SLOTS - 1)], meta_send)
    await_bytes(near.at[pl.ds(1, HALVES * SLOTS - 1)], near_send)
    await_bytes(updated.at[pl.ds(1, SLOTS - 1)], fresh_send)
    await_bytes(updated, fresh_recv)

    await_bytes(last.at[pl.ds(1, HALVES * SLOTS - 1)], last_recv)
    total = last[:SLOTS] + last[SLOTS:]
    for pair in range(CLUSTERS // 2):
        rows = slice(pair * CHUNK, (pair + 1) * CHUNK)
        both = total[:, rows].reshape(nodes, 2 * PIECE).T
        shares[:, 2 * pair, :] = both[:PIECE]
        shares[:, 2 * pair + 1, :] = both[PIECE:]
    await_bytes(last.at[pl.ds(1, HALVES * SLOTS - 1)], last_send)


def on_device(ring, turn_reach, regrets, pot, turn_cluster, bucket_map, codes, ranks):
    width = ranks.shape[1]
    depth = ring * LANES
    near = HALVES * SLOTS
    nodes = SLOTS * CHUNK
    chips = ring // CORES
    tile = (CLUSTERS // 2 * CHUNK, 2 * PIECE)
    vmem = pl.BlockSpec(memory_space=pltpu.VMEM)
    hbm = pl.BlockSpec(memory_space=pltpu.HBM)
    dma = pltpu.SemaphoreType.DMA
    fresh, shares = pl.pallas_call(
        kernel,
        out_shape=(
            jax.ShapeDtypeStruct((nodes, width), jnp.float32),
            jax.ShapeDtypeStruct((PIECE, CLUSTERS, nodes), jnp.float32),
        ),
        in_specs=[hbm, hbm, hbm, hbm, pl.BlockSpec(memory_space=pltpu.SMEM), hbm, hbm],
        out_specs=(hbm, vmem),
        scratch_shapes=[
            pltpu.VMEM((depth, width), SMALL),
            pltpu.VMEM((width, depth), SMALL),
            pltpu.VMEM((width, width), SMALL),
            pltpu.VMEM((PIECE, CLUSTERS, nodes), jnp.bfloat16),
            pltpu.VMEM((PIECE, CLUSTERS, nodes), jnp.float32),
            pltpu.VMEM((SLOTS, *tile), jnp.bfloat16),
            pltpu.VMEM((1, nodes), jnp.float32),
            pltpu.VMEM((1, nodes), jnp.int32),
            pltpu.VMEM((1, width), jnp.int32),
            pltpu.VMEM((1, width), jnp.int32),
            pltpu.VMEM((SLOTS, CHUNK, 2 * LANES), jnp.float32),
            pltpu.VMEM((SLOTS, CHUNK, 2 * LANES), jnp.float32),
            pltpu.VMEM((SLOTS, CHUNK, width), jnp.float32),
            pltpu.VMEM((SLOTS, CHUNK, width), jnp.float32),
            pltpu.VMEM((near, *tile), jnp.bfloat16),
            pltpu.VMEM((1, LANES), jnp.int32),
            pltpu.VMEM((ring, 1, LANES), jnp.int32),
            pltpu.VMEM((ring, ROWS, LANES), jnp.bfloat16),
            pltpu.VMEM((chips, ROWS, CORES * LANES), jnp.bfloat16),
            pltpu.VMEM((ROWS, width), jnp.float32),
            pltpu.VMEM((ROWS, width), jnp.bfloat16),
            pltpu.VMEM((SLOTS, CHUNK, width), jnp.float32),
            pltpu.VMEM((ROWS, width), jnp.bfloat16),
            pltpu.VMEM((chips, ROWS, CORES * LANES), jnp.bfloat16),
            pltpu.VMEM((ring, ROWS, LANES), jnp.bfloat16),
            pltpu.VMEM((near, *tile), jnp.float32),
            pltpu.VMEM((near, *tile), jnp.float32),
            dma((5,)),
            dma,
            dma,
            dma,
            dma,
            dma,
            dma,
            dma,
            dma,
            dma,
            dma((chips,)),
            dma,
            dma,
            dma,
            dma,
            dma,
            dma,
        ],
        compiler_params=pltpu.CompilerParams(
            collective_id=0, has_side_effects=True, vmem_limit_bytes=32 * 2**20
        ),
    )(
        *(
            pltpu.with_memory_space_constraint(x, pltpu.HBM)
            for x in (regrets[0, 0], turn_reach[0], pot[None], codes[None])
        ),
        turn_cluster,
        *(pltpu.with_memory_space_constraint(x, pltpu.HBM) for x in (bucket_map, ranks)),
    )
    return fresh[None, None], shares[None]


def solution(mesh):
    return jax.shard_map(
        functools.partial(on_device, mesh.shape["board"] // HALVES),
        mesh=mesh,
        in_specs=(
            P("pair", "board", None, "hist"),
            P("pair", "board", "hist", None),
            P("hist"),
            P("board"),
            P("board", None),
            P("hist"),
            P("board", None),
        ),
        out_specs=(P("pair", "board", "hist", None), P("pair", "board", None, "hist")),
        check_vma=False,
    )
```

```python
import functools

import jax
import jax.numpy as jnp
from jax import lax
from jax.experimental import pallas as pl
from jax.experimental.pallas import tpu as pltpu
from jax.sharding import PartitionSpec as P

ACTIONS = 4
CLUSTERS = 4
PLAYERS = 2
SMOOTH = 0.01
CHUNK = 8
SLOTS = PLAYERS * ACTIONS
ROWS = SLOTS * CHUNK
HALVES = 2
PIECE = 64
CORES = 2
LANES = 128
MESH = pl.DeviceIdType.MESH
SMALL = jnp.float8_e4m3fn


def times(rows, matrix):
    return lax.dot_general(
        rows, matrix, (((1,), (0,)), ((), ())), preferred_element_type=jnp.float32
    )


def kernel(
    regrets,
    turn_reach,
    pot,
    codes,
    cluster,
    mapping,
    ranks,
    fresh,
    shares,
    onehot,
    spread,
    strength,
    turn_raw,
    turn_rows,
    turn,
    pot_row,
    code_row,
    map_row,
    rank_row,
    meta_out,
    meta,
    regret,
    sigma,
    near,
    cluster_out,
    clusters,
    far_out,
    far,
    lifted,
    reach,
    updated,
    weighted,
    back_out,
    back,
    last_out,
    last,
    fetch_sem,
    regret_send,
    regret_recv,
    meta_send,
    meta_recv,
    near_send,
    near_recv,
    cluster_send,
    cluster_recv,
    far_send,
    far_recv,
    fresh_send,
    fresh_recv,
    back_send,
    back_recv,
    last_send,
    last_recv,
):
    width = ranks.shape[1]
    ring = back.shape[0]
    chips = ring // CORES
    board = lax.axis_index("board")
    action = lax.axis_index("hist")
    player = lax.axis_index("pair")
    half = board // ring
    place = board % ring
    chip = place // CORES
    core = place % CORES
    chunk = action * PLAYERS + player
    slot = player * ACTIONS + action
    scale = width ** (-0.5)
    inward = [(i + 1) // 2 if i % 2 else (chips - i // 2) % chips for i in range(chips)]
    outward = inward[::-1]

    def same_board(step):
        other = (chunk + step) % SLOTS
        return other, {"board": board, "hist": other // PLAYERS, "pair": other % PLAYERS}

    def near_peer(step):
        their_half = (half + step // SLOTS) % HALVES
        their_action = (action + step % SLOTS // PLAYERS) % ACTIONS
        their_player = (player + step) % PLAYERS
        their_chunk = their_action * PLAYERS + their_player
        their_slot = their_player * ACTIONS + their_action
        target = {
            "board": their_half * ring + place,
            "hist": their_action,
            "pair": their_player,
        }
        return their_half, their_chunk, their_slot, target

    def hops(step):
        along = step % SLOTS // PLAYERS
        across = 1 if step % PLAYERS else 2 * (step // SLOTS)
        return min(along, ACTIONS - along) + across

    near_steps = sorted(range(1, HALVES * SLOTS), key=hops, reverse=True)
    far_steps = [
        step
        for distance in outward
        for step in range(distance * CORES, (distance + 1) * CORES)
        if step > 0
    ]

    def far_peer(step):
        there = (chip + step // CORES) % chips
        mate = (core + step) % CORES
        other = there * CORES + mate
        target = {"board": half * ring + other, "hist": action, "pair": player}
        return there, mate, other, target

    def lanes_of(index):
        return pl.ds(pl.multiple_of(index * LANES, LANES), LANES)

    def chunk_of(index):
        return pl.ds(pl.multiple_of(index * CHUNK, CHUNK), CHUNK)

    def remote(src, dst, send, recv, target):
        return pltpu.make_async_remote_copy(
            src_ref=src,
            dst_ref=dst,
            send_sem=send,
            recv_sem=recv,
            device_id=target,
            device_id_type=MESH,
        )

    def await_bytes(buffer, semaphore):
        pltpu.make_async_copy(buffer, buffer, semaphore).wait()

    def regret_copy(step):
        other, target = same_board(step)
        return remote(
            regrets.at[chunk_of(other)], regret.at[slot], regret_send, regret_recv, target
        )

    def meta_copy(step):
        other, target = same_board(step)
        return remote(meta_out.at[other], meta.at[slot], meta_send, meta_recv, target)

    def near_copy(step):
        their_half, their_chunk, their_slot, target = near_peer(step)
        return remote(
            turn.at[their_chunk],
            near.at[half * SLOTS + slot],
            near_send,
            near_recv,
            target,
        )

    def cluster_copy(step):
        there, mate, other, target = far_peer(step)
        return remote(cluster_out, clusters.at[place], cluster_send, cluster_recv, target)

    def far_copy(step):
        there, mate, other, target = far_peer(step)
        return remote(
            far_out.at[other],
            far.at[chip, :, lanes_of(core)],
            far_send,
            far_recv.at[step // CORES],
            target,
        )

    def fresh_copy(step):
        other, target = same_board(step)
        their_slot = (other % PLAYERS) * ACTIONS + other // PLAYERS
        return remote(
            updated.at[their_slot],
            fresh.at[chunk_of(chunk)],
            fresh_send,
            fresh_recv,
            target,
        )

    def back_copy(there, mate):
        target = {"board": half * ring + there * CORES + mate, "hist": action, "pair": player}
        return remote(
            back_out.at[there, :, lanes_of(mate)],
            back.at[place],
            back_send,
            back_recv,
            target,
        )

    def last_copy(there):
        their_half, rest = there // SLOTS, there % SLOTS
        their_action, their_player = rest // PLAYERS, rest % PLAYERS
        their_slot = their_player * ACTIONS + their_action
        target = {
            "board": their_half * ring + place,
            "hist": their_action,
            "pair": their_player,
        }
        return remote(
            last_out.at[their_half * SLOTS + their_slot],
            last.at[half * SLOTS + chunk],
            last_send,
            last_recv,
            target,
        )

    def each(count, action_of):
        def body(step, carry):
            action_of(step)
            return carry

        lax.fori_loop(1, count, body, 0)

    sources = [
        (turn_reach, turn_raw, fetch_sem.at[0]),
        (pot, pot_row, fetch_sem.at[1]),
        (codes, code_row, fetch_sem.at[2]),
        (ranks, rank_row, fetch_sem.at[3]),
        (mapping, map_row, fetch_sem.at[4]),
        (regrets.at[chunk_of(chunk)], regret.at[slot], regret_recv),
    ]
    fetches = [pltpu.make_async_copy(*source) for source in sources]
    fetches[0].start()

    barrier = pltpu.get_barrier_semaphore()

    def greet_near(step):
        target = near_peer(step)[-1]
        pl.semaphore_signal(barrier, inc=1, device_id=target, device_id_type=MESH)

    def greet_far(step):
        target = far_peer(step)[-1]
        pl.semaphore_signal(barrier, inc=1, device_id=target, device_id_type=MESH)

    around = [(min(step // CORES, chips - step // CORES), False, step) for step in far_steps]
    across = [(hops(step), True, step) for step in near_steps]
    merged = sorted(across + around, key=lambda item: -item[0])

    for distance, in_plane, step in merged:
        if in_plane:
            greet_near(step)
        else:
            greet_far(step)
    for fetch in fetches[1:]:
        fetch.start()

    own_cluster = jnp.full((1, LANES), cluster[0], jnp.int32)
    cluster_out[...] = own_cluster
    clusters[place] = own_cluster
    for fetch in fetches[:3]:
        fetch.wait()
    nodes = SLOTS * CHUNK
    turn_rows[...] = turn_raw[...].astype(jnp.float32)
    columns = []
    for pair in range(CLUSTERS // 2):
        both = jnp.concatenate([turn_rows[:, 2 * pair, :], turn_rows[:, 2 * pair + 1, :]], axis=0)
        columns.append(both.T.reshape(SLOTS, CHUNK, 2 * PIECE))
    turn[...] = jnp.concatenate(columns, axis=1).astype(jnp.bfloat16)
    line = lax.broadcasted_iota(jnp.int32, (nodes, nodes), 0)
    column = lax.broadcasted_iota(jnp.int32, (nodes, nodes), 1)
    diagonal = line == column
    pot_rows = jnp.sum(jnp.where(diagonal, pot_row[...], 0.0), axis=1, keepdims=True)
    code_rows = jnp.sum(
        jnp.where(diagonal, code_row[...].astype(jnp.float32), 0.0), axis=1, keepdims=True
    )
    meta_out[:, :, :LANES] = jnp.broadcast_to(pot_rows, (nodes, LANES)).reshape(
        SLOTS, CHUNK, LANES
    )
    meta_out[:, :, LANES:] = jnp.broadcast_to(code_rows, (nodes, LANES)).reshape(
        SLOTS, CHUNK, LANES
    )
    near[half * SLOTS + slot] = turn[chunk]
    meta[slot] = meta_out[chunk]
    pl.semaphore_wait(barrier, HALVES * SLOTS - 1 + ring - 1)

    for distance, in_plane, step in merged:
        if in_plane:
            near_copy(step).start()
        else:
            cluster_copy(step).start()
    each(SLOTS, lambda step: meta_copy(step).start())

    for fetch in fetches[3:5]:
        fetch.wait()
    rank_wide = rank_row[...].astype(jnp.float32)

    def build_strength(block, carry):
        mine = rank_row[:, lanes_of(block)].astype(jnp.float32)
        rank_column = jnp.broadcast_to(mine, (LANES, LANES)).T
        for tile in range(width // LANES):
            span = slice(tile * LANES, (tile + 1) * LANES)
            sign = jnp.minimum(jnp.maximum(rank_wide[:, span] - rank_column, -1.0), 1.0)
            strength[lanes_of(block), span] = sign.astype(SMALL)
        return carry

    lax.fori_loop(0, width // LANES // 2, build_strength, 0)
    each(SLOTS, lambda step: regret_copy(step).start())
    lax.fori_loop(width // LANES // 2, width // LANES, build_strength, 0)


    await_bytes(near.at[pl.ds(1, HALVES * SLOTS - 1)], near_recv)
    await_bytes(clusters.at[pl.ds(1, ring - 1)], cluster_recv)
    low = lax.broadcasted_iota(jnp.int32, (SLOTS, CHUNK, LANES), 2) < PIECE
    parts = []
    lower = near[:SLOTS].astype(jnp.float32)
    upper = near[SLOTS:].astype(jnp.float32)
    for pair in range(CLUSTERS // 2):
        rows = slice(pair * CHUNK, (pair + 1) * CHUNK)
        first, second = lower[:, rows], upper[:, rows]
        parts.append(jnp.where(low, first, pltpu.roll(second, PIECE, 2)))
        parts.append(jnp.where(low, pltpu.roll(first, PIECE, 2), second))
    panels = [part.reshape(ROWS, LANES) for part in parts]

    def choose(other):
        wanted = clusters[other]
        result = panels[0]
        for index in range(1, CLUSTERS):
            result = jnp.where(wanted == index, panels[index], result)
        return result.astype(jnp.bfloat16)

    for step in far_steps:
        other = far_peer(step)[2]
        far_out[other] = choose(other)
        far_copy(step).start()
    far[chip, :, lanes_of(core)] = choose(place)

    bucket = map_row[...]
    shard, within = bucket // PIECE, bucket % PIECE
    map_row[...] = (shard % ring) * LANES + (shard // ring) * PIECE + within
    map_wide = map_row[...]
    tiles = ring * LANES // LANES

    def build_onehot(block, carry):
        index = lax.broadcasted_iota(jnp.int32, (LANES, LANES), 0) + block * LANES
        for tile in range(width // LANES):
            span = slice(tile * LANES, (tile + 1) * LANES)
            hit = jnp.where(map_wide[:, span] == index, 1.0, 0.0)
            onehot[lanes_of(block), span] = hit.astype(SMALL)
        return carry

    lax.fori_loop(0, tiles, build_onehot, 0)

    def build_spread(block, carry):
        mine = map_row[:, lanes_of(block)].astype(jnp.float32)
        map_column = jnp.broadcast_to(mine, (LANES, LANES)).T.astype(jnp.int32)
        index = lax.broadcasted_iota(jnp.int32, (LANES, LANES), 1)
        for tile in range(tiles):
            span = slice(tile * LANES, (tile + 1) * LANES)
            hit = jnp.where(map_column == index + tile * LANES, 1.0, 0.0)
            spread[lanes_of(block), span] = hit.astype(SMALL)
        return carry

    lax.fori_loop(0, width // LANES, build_spread, 0)

    step_width = min(512, width)
    spans = [slice(first, first + step_width) for first in range(0, width, step_width)]

    def match(span):
        for who in range(PLAYERS):
            positive = [
                jnp.maximum(regret[who * ACTIONS + act, :, span], 0.0) for act in range(ACTIONS)
            ]
            total = (positive[0] + positive[1]) + (positive[2] + positive[3])
            inverse = 1.0 / (total + ACTIONS * SMOOTH)
            for act in range(ACTIONS):
                sigma[who * ACTIONS + act, :, span] = (positive[act] + SMOOTH) * inverse

    totals = jnp.zeros((ROWS, 1), jnp.float32)
    for turn_of, distance in enumerate([0] + outward[:-1]):
        if turn_of == chips // 2:
            await_bytes(regret, regret_recv)
            for span in spans:
                match(span)
        arrived = far.at[0, :, pl.ds(0, LANES)] if distance == 0 else far.at[0]
        await_bytes(arrived, far_recv.at[distance])
        source = (chip + chips - distance) % chips
        rows = pl.ds(pl.multiple_of(source * CORES * LANES, CORES * LANES), CORES * LANES)
        panel = far[source]
        for span in spans:
            now = times(panel, onehot[rows, span])
            if turn_of > 0:
                now = now + lifted[:, span]
            if turn_of < chips - 1:
                lifted[:, span] = now
            else:
                now = (now * sigma[:, :, span].reshape(ROWS, step_width)).astype(jnp.bfloat16)
                reach[:, span] = now
                totals = totals + jnp.sum(now.astype(jnp.float32), axis=1, keepdims=True)

    def opponent(rows):
        return jnp.concatenate([rows[ROWS // 2 :], rows[: ROWS // 2]], axis=0)

    await_bytes(meta.at[pl.ds(1, SLOTS - 1)], meta_recv)
    pot_here = meta[:, :, :LANES].reshape(ROWS, LANES) * scale
    code_here = meta[:, :, LANES:].reshape(ROWS, LANES)
    row = lax.broadcasted_iota(jnp.int32, (ROWS, LANES), 0)
    who_here = jnp.where(row >= ROWS // 2, 1.0, 0.0)
    signed = jnp.where(code_here == who_here, -pot_here, pot_here)
    fold = signed * opponent(totals)
    repeats = step_width // LANES
    fold_wide = jnp.concatenate([fold] * repeats, axis=1)
    pot_wide = jnp.concatenate([pot_here] * repeats, axis=1)
    show_wide = jnp.concatenate([code_here] * repeats, axis=1) == 2.0

    for span in spans:
        equity = times(reach[...], strength[:, span])
        value = jnp.where(show_wide, pot_wide * opponent(equity), fold_wide)
        updated[:, :, span] = value.reshape(SLOTS, CHUNK, step_width)
        share = sigma[:, :, span].reshape(ROWS, step_width) * value
        weighted[:, span] = share.astype(jnp.bfloat16)

    def renew(tile, carry):
        span = lanes_of(tile)
        for who in range(PLAYERS):
            those = [who * ACTIONS + act for act in range(ACTIONS)]
            value = [updated[index, :, span] for index in those]
            share = [sigma[index, :, span] * now for index, now in zip(those, value)]
            node = (share[0] + share[1]) + (share[2] + share[3])
            for index, now in zip(those, value):
                updated[index, :, span] = (regret[index, :, span] + now) - node
        return carry

    keep_fresh = pltpu.make_async_copy(updated.at[slot], fresh.at[chunk_of(chunk)], fresh_recv)

    for turn_of, there in enumerate([0, 1, 2, 3, 4, 5, 6, 7]):
        if turn_of == chips // 2:
            lax.fori_loop(0, width // LANES, renew, 0)
            each(SLOTS, lambda step: fresh_copy(step).start())
            keep_fresh.start()
        columns_there = slice(there * CORES * LANES, (there + 1) * CORES * LANES)
        block = times(weighted[...], spread[:, columns_there])
        back_out[there] = block.astype(jnp.bfloat16)
        if turn_of % 2:
            for one, mate in ((there - 1, 1), (there, 1), (there - 1, 0), (there, 0)):

                @pl.when(place != one * CORES + mate)
                def send_back(one=one, mate=mate):
                    back_copy(one, mate).start()

    back[place] = back_out[chip, :, lanes_of(core)]

    held = [jnp.zeros((ROWS, LANES), jnp.float32) for unused in range(CLUSTERS)]
    await_bytes(back.at[pl.ds(1, ring - 1)], back_recv)
    for source in range(ring):
        block = back[source].astype(jnp.float32)
        theirs = clusters[source]
        for index in range(CLUSTERS):
            held[index] = held[index] + jnp.where(theirs == index, block, 0.0)
    held = [part.reshape(SLOTS, CHUNK, LANES) for part in held]
    def lateness(there):
        return there // SLOTS * PLAYERS + there % PLAYERS + there % SLOTS // PLAYERS

    for their_half in range(HALVES):
        for pair in range(CLUSTERS // 2):
            rows = slice(pair * CHUNK, (pair + 1) * CHUNK)
            first, second = held[2 * pair], held[2 * pair + 1]
            if their_half == 0:
                piece = jnp.where(low, first, pltpu.roll(second, PIECE, 2))
            else:
                piece = jnp.where(low, pltpu.roll(first, PIECE, 2), second)
            last_out[their_half * SLOTS : (their_half + 1) * SLOTS, rows] = piece
        theirs = range(their_half * SLOTS, (their_half + 1) * SLOTS)
        for there in sorted(theirs, key=lateness):

            @pl.when(there != half * SLOTS + chunk)
            def send_last(there=there):
                last_copy(there).start()

    last[half * SLOTS + chunk] = last_out[half * SLOTS + slot]

    await_bytes(clusters.at[pl.ds(1, ring - 1)], cluster_send)
    await_bytes(far_out.at[pl.ds(1, ring - 1)], far_send)
    await_bytes(back.at[pl.ds(1, ring - 1)], back_send)
    await_bytes(regret.at[pl.ds(1, SLOTS - 1)], regret_send)
    await_bytes(meta.at[pl.ds(1, SLOTS - 1)], meta_send)
    await_bytes(near.at[pl.ds(1, HALVES * SLOTS - 1)], near_send)
    await_bytes(updated.at[pl.ds(1, SLOTS - 1)], fresh_send)
    await_bytes(updated, fresh_recv)

    await_bytes(last.at[pl.ds(1, HALVES * SLOTS - 1)], last_recv)
    total = last[:SLOTS] + last[SLOTS:]
    for pair in range(CLUSTERS // 2):
        rows = slice(pair * CHUNK, (pair + 1) * CHUNK)
        both = total[:, rows].reshape(nodes, 2 * PIECE).T
        shares[:, 2 * pair, :] = both[:PIECE]
        shares[:, 2 * pair + 1, :] = both[PIECE:]
    await_bytes(last.at[pl.ds(1, HALVES * SLOTS - 1)], last_send)


def on_device(ring, turn_reach, regrets, pot, turn_cluster, bucket_map, codes, ranks):
    width = ranks.shape[1]
    depth = ring * LANES
    near = HALVES * SLOTS
    nodes = SLOTS * CHUNK
    chips = ring // CORES
    tile = (CLUSTERS // 2 * CHUNK, 2 * PIECE)
    vmem = pl.BlockSpec(memory_space=pltpu.VMEM)
    hbm = pl.BlockSpec(memory_space=pltpu.HBM)
    dma = pltpu.SemaphoreType.DMA
    fresh, shares = pl.pallas_call(
        kernel,
        out_shape=(
            jax.ShapeDtypeStruct((nodes, width), jnp.float32),
            jax.ShapeDtypeStruct((PIECE, CLUSTERS, nodes), jnp.float32),
        ),
        in_specs=[hbm, hbm, hbm, hbm, pl.BlockSpec(memory_space=pltpu.SMEM), hbm, hbm],
        out_specs=(hbm, vmem),
        scratch_shapes=[
            pltpu.VMEM((depth, width), SMALL),
            pltpu.VMEM((width, depth), SMALL),
            pltpu.VMEM((width, width), SMALL),
            pltpu.VMEM((PIECE, CLUSTERS, nodes), jnp.bfloat16),
            pltpu.VMEM((PIECE, CLUSTERS, nodes), jnp.float32),
            pltpu.VMEM((SLOTS, *tile), jnp.bfloat16),
            pltpu.VMEM((1, nodes), jnp.float32),
            pltpu.VMEM((1, nodes), jnp.int32),
            pltpu.VMEM((1, width), jnp.int32),
            pltpu.VMEM((1, width), jnp.int32),
            pltpu.VMEM((SLOTS, CHUNK, 2 * LANES), jnp.float32),
            pltpu.VMEM((SLOTS, CHUNK, 2 * LANES), jnp.float32),
            pltpu.VMEM((SLOTS, CHUNK, width), jnp.float32),
            pltpu.VMEM((SLOTS, CHUNK, width), jnp.float32),
            pltpu.VMEM((near, *tile), jnp.bfloat16),
            pltpu.VMEM((1, LANES), jnp.int32),
            pltpu.VMEM((ring, 1, LANES), jnp.int32),
            pltpu.VMEM((ring, ROWS, LANES), jnp.bfloat16),
            pltpu.VMEM((chips, ROWS, CORES * LANES), jnp.bfloat16),
            pltpu.VMEM((ROWS, width), jnp.float32),
            pltpu.VMEM((ROWS, width), jnp.bfloat16),
            pltpu.VMEM((SLOTS, CHUNK, width), jnp.float32),
            pltpu.VMEM((ROWS, width), jnp.bfloat16),
            pltpu.VMEM((chips, ROWS, CORES * LANES), jnp.bfloat16),
            pltpu.VMEM((ring, ROWS, LANES), jnp.bfloat16),
            pltpu.VMEM((near, *tile), jnp.float32),
            pltpu.VMEM((near, *tile), jnp.float32),
            dma((5,)),
            dma,
            dma,
            dma,
            dma,
            dma,
            dma,
            dma,
            dma,
            dma,
            dma((chips,)),
            dma,
            dma,
            dma,
            dma,
            dma,
            dma,
        ],
        compiler_params=pltpu.CompilerParams(
            collective_id=0, has_side_effects=True, vmem_limit_bytes=32 * 2**20
        ),
    )(
        *(
            pltpu.with_memory_space_constraint(x, pltpu.HBM)
            for x in (regrets[0, 0], turn_reach[0], pot[None], codes[None])
        ),
        turn_cluster,
        *(pltpu.with_memory_space_constraint(x, pltpu.HBM) for x in (bucket_map, ranks)),
    )
    return fresh[None, None], shares[None]


def solution(mesh):
    return jax.shard_map(
        functools.partial(on_device, mesh.shape["board"] // HALVES),
        mesh=mesh,
        in_specs=(
            P("pair", "board", None, "hist"),
            P("pair", "board", "hist", None),
            P("hist"),
            P("board"),
            P("board", None),
            P("hist"),
            P("board", None),
        ),
        out_specs=(P("pair", "board", "hist", None), P("pair", "board", None, "hist")),
        check_vma=False,
    )
```
